512 devices in a mesh: group: 16 (over y, x_lo), fsdp: 32 (over x_hi, z, core).
Axes of the slice: x: 4 (x_hi: 2, x_lo: 2; x = x_hi * 2 + x_lo), y: 8, z: 8, core: 2. Of those that a mesh axis runs over, the one named last changes fastest.
Arguments:
- grad_terms: bfloat16 [16, 32, 64, 8192], P('group', 'fsdp'), may hold values from -0.59765625 to 0.59765625
- master: float32 [64, 8192], P('fsdp'), may hold values from -6 to 6
- inner_drift: float32 [16, 64, 8192], P('group', 'fsdp'), may hold values from -0.6 to 0.6
- momentum: float32 [64, 8192], P('fsdp'), may hold values from -3 to 3
- moment_codes: int32 [16, 64, 8192], P('group', 'fsdp'), may hold values from 0 to 255
- second_codes: int32 [16, 64, 8192], P('group', 'fsdp'), may hold values from 0 to 255
- moment_scale: float32 [16, 64, 32], P('group', 'fsdp'), may hold values from 0.01 to 0.1
- second_scale: float32 [16, 64, 32], P('group', 'fsdp'), may hold values from 0.05 to 0.5
- counts: int32 [16], P('group'), may hold values from 256 to 6144, as said below
Outputs:
- master_new: float32 [64, 8192], P('fsdp')
- momentum_new: float32 [64, 8192], P('fsdp')
- moment_new: float32 [16, 64, 8192], P('group', 'fsdp')
- second_new: float32 [16, 64, 8192], P('group', 'fsdp')
- model_copy: bfloat16 [64, 8192], replicated
The draws below stay inside these ranges and needn't reach their ends.
Inputs may be any that keep to these rules, and one draw needn't show every extreme that they name: `counts`: one group trained on 6144 tokens, every other on 256 to 2048.
All inputs are finite; a program needn't handle non-finite values.
Results may differ from the reference program's by a relative error of at most 0.0004.
Values may be sent and summed in bfloat16 or wider, within the bound.
A program may use at most 64 MiB of HBM per device.

```python
import math
import jax
import jax.numpy as jnp
from jax import lax

D = 8192
ROWS = 64
BLOCK = 256
STEP = 500
N_GROUP = 16
N_FSDP = 32


def draw_counts(key, part):
    folded = jax.random.fold_in(key, 7)
    first_key, second_key = jax.random.split(folded)
    base = jax.random.randint(first_key, (N_GROUP,), 256, 2049)
    chosen = jax.random.randint(second_key, (), 0, N_GROUP)
    return jnp.where(jnp.arange(N_GROUP) == chosen, 6144, base).astype(jnp.int32)


def with_ends(values, own_key, low, high):
    dims = values.shape
    spot = [jax.random.randint(jax.random.fold_in(own_key, axis), (), 0, dims[axis]) for axis in range(len(dims))]
    values = values.at[tuple(spot)].set(low)
    longest = dims.index(max(dims))
    spot[longest] = (spot[longest] + 1) % dims[longest]
    return values.at[tuple(spot)].set(high)


def with_spikes(values, key, source, target, blocks, factor):
    owner, partner = [(jnp.arange(values.shape[axis_at]) // (values.shape[axis_at] // blocks)).reshape([-1 if axis == axis_at else 1 for axis in range(values.ndim)]) for axis_at in (source, target)]
    chosen = jax.random.permutation(key, blocks)[partner]
    strong = (owner == chosen) | (owner == (partner + blocks // 2) % blocks)
    return jnp.where(strong, factor * values, values)


def block_levels(own_key, shape, shards, low, high):
    def one(position, shards_of):
        draws = jax.random.uniform(jax.random.fold_in(jax.random.fold_in(own_key, 6), position), (shards_of,), jnp.float32, low / len(shards), high / len(shards))
        return jnp.repeat(jnp.exp(draws), shape[position] // shards_of).reshape((-1,) + (1,) * (len(shape) - position - 1))

    level = one(*shards[0])
    for cut in shards[1:]:
        level = level * one(*cut)
    return level


def gaussian(rng, shape, deviation, bound, cuts=(), kind=jnp.bfloat16):
    factor_of = block_levels(rng, shape, cuts, -0.22, 0.18) if cuts else 1.0
    result = jax.random.normal(rng, shape, jnp.float32) * deviation * factor_of
    return jnp.minimum(jnp.maximum(result, -bound), bound).astype(kind)


def heavy_noise(rng, shape, spread, limit, cuts, heavy, held_as=jnp.bfloat16):
    result = spread * jax.random.normal(rng, shape, jnp.float32)
    if cuts:
        result = result * block_levels(rng, shape, cuts, -0.22, 0.18)
    return jnp.clip(with_spikes(result, jax.random.fold_in(rng, 3), *heavy), -limit, limit).astype(held_as)


def setup_inputs(seed: int = 0) -> dict:
    key_list = jax.random.split(jax.random.key(seed), 10)
    return {
        "grad_terms": heavy_noise(key_list[0], (N_GROUP, N_FSDP, ROWS, D), 0.1, 0.59765625, ((0, 16), (1, 32)), (1, 2, 32, 2.75)),
        "master": gaussian(key_list[1], (ROWS, D), 1.0, 6.0, ((0, 32),), jnp.float32),
        "inner_drift": gaussian(key_list[2], (N_GROUP, ROWS, D), 0.1, 0.6, ((0, 16), (1, 32)), jnp.float32),
        "momentum": gaussian(key_list[3], (ROWS, D), 0.5, 3.0, ((0, 32),), jnp.float32),
        "moment_codes": with_ends(jax.random.randint(key_list[4], (N_GROUP, ROWS, D), 0, 256), jax.random.fold_in(key_list[4], 1), 0, 255).astype(jnp.int32),
        "second_codes": with_ends(jax.random.randint(key_list[5], (N_GROUP, ROWS, D), 0, 256), jax.random.fold_in(key_list[5], 1), 0, 255).astype(jnp.int32),
        "moment_scale": jnp.clip(jnp.exp(math.log(0.1) - 2.3025851 * jax.random.uniform(key_list[6], (N_GROUP, ROWS, D // BLOCK), jnp.float32) ** block_levels(key_list[6], (N_GROUP, ROWS, D // BLOCK), ((0, 16), (1, 32)), -0.2, 0.2)), 0.01, 0.1),
        "second_scale": jnp.clip(jnp.exp(math.log(0.5) - 2.3025851 * jax.random.uniform(key_list[7], (N_GROUP, ROWS, D // BLOCK), jnp.float32) ** block_levels(key_list[7], (N_GROUP, ROWS, D // BLOCK), ((0, 16), (1, 32)), -0.2, 0.2)), 0.05, 0.5),
        "counts": draw_counts(jax.random.fold_in(key_list[9], 71), 0),
    }


def blockwise(values, scale):
    shaped = values.reshape(values.shape[:-1] + (values.shape[-1] // BLOCK, BLOCK))
    return (shaped * scale[..., None]).reshape(values.shape)

def reference(grad_terms, master, inner_drift, momentum, moment_codes, second_codes, moment_scale, second_scale, counts):
    grad = lax.map(lambda terms: lax.optimization_barrier(jnp.sum(terms.astype(jnp.float32), axis=0)), grad_terms)
    signed = (moment_codes.astype(jnp.float32) - 127.5) / 127.5
    moment_old = blockwise(signed * signed * signed, moment_scale)
    unsigned = (second_codes.astype(jnp.float32) + 16.0) / 271.0
    second_old = blockwise(unsigned * unsigned, second_scale)
    moment_new = 0.9 * moment_old + 0.1 * grad
    second_new = 0.999 * second_old + 0.001 * grad * grad
    update = moment_new / (1.0 - 0.9 ** STEP) / (jnp.sqrt(second_new / (1.0 - 0.999 ** STEP)) + 1e-08)
    inner = master[None] + inner_drift
    pseudo = master[None] - (inner - 0.8 * (update + 0.025 * inner))
    weights = counts.astype(jnp.float32)
    mean_pseudo = lax.optimization_barrier(jnp.sum(weights[:, None, None] * pseudo, axis=0)) / jnp.sum(weights)
    momentum_new = 0.9 * momentum + mean_pseudo
    master_new = master - 0.7 * (mean_pseudo + 0.9 * momentum_new)
    return (master_new, momentum_new, moment_new, second_new, master_new.astype(jnp.bfloat16))
```

```python
import jax
import jax.numpy as jnp
from jax import lax
from jax.experimental import pallas as pl
from jax.experimental.pallas import tpu as pltpu
from jax.sharding import PartitionSpec as P

BLOCK = 256
STEP = 500
MESH = pl.DeviceIdType.MESH
F32 = jnp.float32
CODE = 27408.0


def far_first(i):
    j = i // 2
    off = jnp.where(j % 2 == 1, 8 - (j + 1) // 2, j // 2)
    return (4 + off) % 8, 1 - i % 2


def place():
    g = lax.axis_index("group")
    f = lax.axis_index("fsdp")
    return g // 2, g % 2, f // 16, (f // 2) % 8, f % 2


def fsdp_peer(i, sign, xh, z, core):
    dz, dx = far_first(i)
    return (xh + dx) % 2, (z + 8 + sign * dz) % 8


def group_peer(i, sign, y, xl):
    dy, dx = far_first(i)
    return ((y + 8 + sign * dy) % 8) * 2 + (xl + dx) % 2


def kernel(
    grad, master, drift, mom, mcode, scode, mscale, sscale, counts,
    o_master, o_mom, o_m, o_s, o_model,
    loc, sib, out_code, in_code, old_m, old_s, weighted, part, mean, w_out, w_in,
    new_master, new_mom, new_m, new_s, copy16, in16,
    s_loc, s_sib, r_sib, s_code, r_code, s_w, r_w, s_part, r_part, s_mean, r_mean, s_mod, r_mod,
    s_fwd, r_fwd, s_own, s_out,
):
    y, xl, xh, z, core = place()
    me_g = y * 2 + xl
    me_f = xh * 16 + z * 2 + core
    sibling = (me_g, me_f + 1 - 2 * core)

    def chip(i, sign=1):
        px, pz = fsdp_peer(i, sign, xh, z, core)
        return px * 4 + pz // 2, pz % 2, (me_g, px * 16 + pz * 2 + core)

    def peer(i):
        return (group_peer(i, 1, y, xl), me_f)

    barrier = pltpu.get_barrier_semaphore()
    pl.semaphore_signal(barrier, inc=1, device_id=sibling, device_id_type=MESH)

    def greet(i, _):
        pl.semaphore_signal(barrier, inc=1, device_id=chip(i)[2], device_id_type=MESH)
        pl.semaphore_signal(barrier, inc=1, device_id=peer(i), device_id_type=MESH)
        return 0

    lax.fori_loop(0, 15, greet, 0)

    def local_copy(i):
        t, par, _ = chip(i)
        return pltpu.make_async_copy(grad.at[t, :, par * 2 + core], loc.at[i], s_loc.at[i])

    def sibling_copy(i):
        t, par, _ = chip(i)
        return pltpu.make_async_remote_copy(
            grad.at[t, :, par * 2 + 1 - core], sib.at[i], s_sib.at[i], r_sib.at[i],
            device_id=sibling, device_id_type=MESH,
        )

    def code_copy(i):
        return pltpu.make_async_remote_copy(
            out_code.at[i], in_code.at[i], s_code.at[i], r_code.at[i],
            device_id=chip(i)[2], device_id_type=MESH,
        )

    def w_copy(i):
        return pltpu.make_async_remote_copy(
            w_out, w_in.at[i], s_w.at[i], r_w.at[i], device_id=peer(i), device_id_type=MESH
        )

    def part_copy(i):
        to = group_peer(i, 1, y, xl)
        return pltpu.make_async_remote_copy(
            weighted.at[pl.ds(pl.multiple_of(to * 8, 8), 8)], part.at[i], s_part.at[i], r_part.at[i],
            device_id=(to, me_f), device_id_type=MESH,
        )

    mine = pl.ds(pl.multiple_of(me_g * 8, 8), 8)

    def mean_copy(i, source):
        at = pl.ds(pl.multiple_of(source * 8, 8), 8)
        return pltpu.make_async_remote_copy(
            mean.at[at], mean.at[at], s_mean.at[i], r_mean.at[i], device_id=peer(i), device_id_type=MESH
        )

    def model_copy(i):
        return pltpu.make_async_remote_copy(
            copy16, in16.at[i], s_mod.at[i], r_mod.at[i], device_id=chip(i)[2], device_id_type=MESH
        )

    def row_at(i):
        t, par, _ = chip(i, -1)
        return t, par * 2

    def own_store(i, source):
        t, s = row_at(i)
        return pltpu.make_async_copy(source, o_model.at[t, :, s + core], s_own.at[i])

    def forward(i, source, whose):
        t, s = row_at(i)
        return pltpu.make_async_remote_copy(
            source, o_model.at[t, :, s + whose], s_fwd.at[i], r_fwd.at[i],
            device_id=sibling, device_id_type=MESH,
        )

    def each(n, f):
        def body(i, _):
            f(i)
            return 0

        lax.fori_loop(0, n, body, 0)

    each(16, lambda i: local_copy(i).start())
    weight = counts[0].astype(F32)
    w_out[...] = jnp.full((8, 128), weight, F32)

    rows = lax.broadcasted_iota(jnp.int32, (128, 32), 0)
    hit = lax.broadcasted_iota(jnp.int32, (128, 32), 1) == rows // 4

    def scale_of(ref):
        both = jnp.where(rows % 2 == 0, ref[0, 0:1, :], ref[0, 1:2, :])
        return jnp.sum(jnp.where(hit, both, 0.0), axis=1, keepdims=True)

    signed = (mcode[...].astype(F32) - 127.5) / 127.5
    old_m[...] = 0.9 * (signed * signed * signed * scale_of(mscale))
    unsigned = (scode[...].astype(F32) + 16.0) / 271.0
    old_s[...] = 0.999 * (unsigned * unsigned * scale_of(sscale))

    pl.semaphore_wait(barrier, 31)
    each(16, lambda i: sibling_copy(i).start())
    each(15, lambda i: w_copy(i).start())

    def pair(i):
        local_copy(i).wait()
        sibling_copy(i).wait_recv()
        return (
            loc.at[i].reshape(128, 128)[...].astype(F32) + sib.at[i].reshape(128, 128)[...].astype(F32)
        )

    def encode(i):
        out_code[i] = jnp.round(pair(i) * CODE).astype(jnp.int32).astype(jnp.int16)
        code_copy(i).start()

    each(15, encode)
    own = pair(15)

    def decode(i, total):
        code_copy(i).wait_recv()
        return total + in_code[i].astype(jnp.int32)

    total = lax.fori_loop(0, 15, decode, jnp.zeros((128, 128), jnp.int32))
    g = own + total.astype(F32) * (1.0 / CODE)
    moment = old_m[...] + 0.1 * g
    second = old_s[...] + 0.001 * g * g
    new_m[...] = moment
    new_s[...] = second
    update = moment / (1.0 - 0.9**STEP) / (jnp.sqrt(second / (1.0 - 0.999**STEP)) + 1e-08)
    inner = master[...] + drift[...]
    pseudo = master[...] - (inner - 0.8 * (update + 0.025 * inner))
    weighted[...] = weight * pseudo

    each(15, lambda i: part_copy(i).start())
    out_m = pltpu.make_async_copy(new_m, o_m, s_out.at[0])
    out_s = pltpu.make_async_copy(new_s, o_s, s_out.at[1])
    out_m.start()
    out_s.start()

    def add_weight(i, total):
        w_copy(i).wait_recv()
        return total + w_in[i]

    all_weights = lax.fori_loop(0, 15, add_weight, w_out[...])

    def add_part(i, total):
        part_copy(i).wait_recv()
        return total + part[i]

    mean[mine, :] = lax.fori_loop(0, 15, add_part, weighted[mine, :]) / all_weights
    each(15, lambda i: mean_copy(i, me_g).start())
    each(15, lambda i: mean_copy(i, group_peer(i, -1, y, xl)).wait_recv())

    momentum = 0.9 * mom[...] + mean[...]
    fresh = master[...] - 0.7 * (mean[...] + 0.9 * momentum)
    copy16.reshape(128, 128)[...] = fresh.astype(jnp.bfloat16)
    each(15, lambda i: model_copy(i).start())
    own_store(15, copy16).start()
    forward(15, copy16, core).start()
    new_mom[...] = momentum
    new_master[...] = fresh
    out_mom = pltpu.make_async_copy(new_mom, o_mom, s_out.at[2])
    out_master = pltpu.make_async_copy(new_master, o_master, s_out.at[3])
    out_mom.start()
    out_master.start()

    def pass_on(i):
        model_copy(i).wait_recv()
        forward(i, in16.at[i], core).start()
        own_store(i, in16.at[i]).start()

    each(15, pass_on)

    def finish(i):
        sibling_copy(i).wait_send()
        forward(i, copy16, core).wait_send()
        forward(i, copy16, 1 - core).wait_recv()
        own_store(i, copy16).wait()

    each(16, finish)

    def finish_sends(i):
        code_copy(i).wait_send()
        w_copy(i).wait_send()
        part_copy(i).wait_send()
        mean_copy(i, me_g).wait_send()
        model_copy(i).wait_send()

    each(15, finish_sends)
    out_m.wait()
    out_s.wait()
    out_mom.wait()
    out_master.wait()


def outer_step(*args):
    any_space = pl.BlockSpec(memory_space=pl.ANY)
    vmem = pl.BlockSpec(memory_space=pltpu.VMEM)
    flat = jax.ShapeDtypeStruct((128, 128), F32)
    dma = pltpu.SemaphoreType.DMA
    rows16 = lambda n: pltpu.VMEM((n, 64, 2, 128), jnp.bfloat16)
    square = pltpu.VMEM((128, 128), F32)
    return pl.pallas_call(
        kernel,
        out_shape=(flat, flat, flat, flat, jax.ShapeDtypeStruct((8, 64, 4, 2, 128), jnp.bfloat16)),
        in_specs=[any_space] + [vmem] * 7 + [pl.BlockSpec(memory_space=pltpu.SMEM)],
        out_specs=(any_space,) * 5,
        scratch_shapes=[
            rows16(16), rows16(16),
            pltpu.VMEM((15, 128, 128), jnp.int16), pltpu.VMEM((15, 128, 128), jnp.int16),
            square, square, square, pltpu.VMEM((15, 8, 128), F32), square,
            pltpu.VMEM((8, 128), F32), pltpu.VMEM((15, 8, 128), F32),
            square, square, square, square,
            pltpu.VMEM((64, 2, 128), jnp.bfloat16), rows16(15),
            dma((16,)), dma((16,)), dma((16,)), dma((15,)), dma((15,)), dma((15,)), dma((15,)),
            dma((15,)), dma((15,)), dma((15,)), dma((15,)), dma((15,)), dma((15,)),
            dma((16,)), dma((16,)), dma((16,)), dma((4,)),
        ],
        compiler_params=pltpu.CompilerParams(
            collective_id=0, has_side_effects=True, vmem_limit_bytes=16 * 1024 * 1024
        ),
        name="outer_step",
    )(*args)


def hand_over(*refs):
    sems = refs[-1]
    copies = [pltpu.make_async_copy(refs[k], refs[5 + k], sems.at[k]) for k in (4, 0, 1, 2, 3)]
    for c in copies:
        c.start()
    for c in copies:
        c.wait()


def on_device(grad_terms, master, inner_drift, momentum, moment_codes, second_codes, moment_scale, second_scale, counts):
    def to_flat(x):
        return x.reshape(2, 64, 128).transpose(1, 0, 2).reshape(128, 128)

    def from_flat(x):
        return x.reshape(64, 2, 128).transpose(1, 0, 2).reshape(2, 8192)

    grad = grad_terms.reshape(8, 4, 2, 64, 128).transpose(0, 3, 1, 2, 4)
    outs = outer_step(
        grad, to_flat(master), to_flat(inner_drift), to_flat(momentum),
        to_flat(moment_codes), to_flat(second_codes), moment_scale, second_scale, counts,
    )
    any_space = pl.BlockSpec(memory_space=pl.ANY)
    a, b, c, d, e = pl.pallas_call(
        hand_over,
        out_shape=tuple(jax.ShapeDtypeStruct(o.shape, o.dtype) for o in outs),
        in_specs=[any_space] * 5,
        out_specs=(any_space,) * 5,
        scratch_shapes=[pltpu.SemaphoreType.DMA((5,))],
        name="hand_over",
    )(*outs)
    return (
        from_flat(a), from_flat(b), from_flat(c)[None], from_flat(d)[None],
        e.transpose(0, 2, 3, 1, 4).reshape(64, 8192),
    )


def solution(mesh):
    rows = P("fsdp", None)
    both = P("group", "fsdp", None)
    return jax.shard_map(
        on_device,
        mesh=mesh,
        in_specs=(P("group", "fsdp", None, None), rows, both, rows, both, both, both, both, P("group")),
        out_specs=(rows, rows, both, both, P()),
        check_vma=False,
    )
```

```python
import jax
import jax.numpy as jnp
from jax import lax
from jax.experimental import pallas as pl
from jax.experimental.pallas import tpu as pltpu
from jax.sharding import PartitionSpec as P

BLOCK = 256
STEP = 500
MESH = pl.DeviceIdType.MESH
F32 = jnp.float32
BF16 = jnp.bfloat16
CODE = 27408.0
RING = (4, 3, 5, 2, 6, 1, 7, 0)
PEERS = tuple((dy, dx) for dy in RING for dx in (1, 0))[:15]


def kernel(
    grad, master_in, drift_in, mom_in, mcode_in, scode_in, mscale_in, sscale_in, counts,
    o_master, o_mom, o_m, o_s, o_model,
    terms, sib, master, drift, mom, mcode, scode, mscale, sscale,
    pairs, out_code, in_code, summed, old_m, old_s, weighted, part, mean, w_out, w_in, order, slice_out, slice_in,
    s_in, s_sib, r_sib, s_code, r_code, s_w, r_w, s_part, r_part, s_mean, r_mean, s_slice, r_slice, s_block, r_block,
    s_fwd, r_fwd,
):
    g = lax.axis_index("group")
    f = lax.axis_index("fsdp")
    y, xl = g // 2, g % 2
    xh, z, core = f // 16, (f // 2) % 8, f % 2
    other = 1 - core
    across = (xh + core) % 2
    zs = [lax.rem(z + d, 8) for d in range(8)]
    ys = [lax.rem(y + d, 8) * 2 for d in range(8)]
    back_ys = [lax.rem(y + 8 - d, 8) * 2 for d in range(8)]
    xls = [xl, 1 - xl]

    def at(px, pz, pc):
        return (g, px * 16 + pz * 2 + pc)

    sibling = at(xh, z, other)

    def remote(source, target, send, recv, device):
        return pltpu.make_async_remote_copy(
            source, target, send, recv, device_id=device, device_id_type=MESH
        )

    loads = [
        pltpu.make_async_copy(grad.at[pl.ds(16 * k, 16)], terms.at[pl.ds(16 * k, 16)], s_in.at[k])
        for k in range(4)
    ]
    small = [
        pltpu.make_async_copy(a, b, s_in.at[4 + k])
        for k, (a, b) in enumerate((
            (mscale_in, mscale), (sscale_in, sscale), (mcode_in, mcode), (scode_in, scode),
            (master_in, master), (drift_in, drift), (mom_in, mom),
        ))
    ]
    for c in loads + small:
        c.start()

    barrier = pltpu.get_barrier_semaphore()

    def greet(device):
        pl.semaphore_signal(barrier, inc=1, device_id=device, device_id_type=MESH)

    for d in RING:
        greet(at(1 - core, zs[d], xh))
        greet(at(core, zs[d], 1 - core))
        if d:
            greet(at(core, zs[d], core))
    pl.when(across == 1)(lambda: greet(at(core, z, core)))
    for dy, dx in PEERS:
        greet((ys[dy] + xls[dx], f))

    for c in small[:4]:
        c.wait()
    weight = counts[0].astype(F32)
    w_out[...] = jnp.full((8, 128), weight, F32)
    rows = lax.broadcasted_iota(jnp.int32, (128, 32), 0)
    hit = lax.broadcasted_iota(jnp.int32, (128, 32), 1) == rows // 4

    def scale_of(ref):
        both = jnp.where(rows % 2 == 0, ref[0, 0:1, :], ref[0, 1:2, :])
        return jnp.sum(jnp.where(hit, both, 0.0), axis=1, keepdims=True)

    signed = (mcode[...].astype(F32) - 127.5) / 127.5
    old_m[...] = 0.9 * (signed * signed * signed * scale_of(mscale))
    unsigned = (scode[...].astype(F32) + 16.0) / 271.0
    old_s[...] = 0.999 * (unsigned * unsigned * scale_of(sscale))
    for c in loads:
        c.wait()

    pl.semaphore_wait(barrier, 38 + across)

    halves = [1 - z // 4, z // 4]

    def half_rows(owner, k):
        return pl.ds(pl.multiple_of(owner * 32 + halves[k] * 16, 16), 16)

    swaps = [
        remote(terms.at[half_rows(other, k)], sib.at[k], s_sib.at[k], r_sib.at[k], sibling) for k in range(2)
    ]
    for c in swaps:
        c.start()

    group_at = [ys[dy] + xls[dx] for dy, dx in PEERS]
    group_from = [back_ys[dy] + xls[dx] for dy, dx in PEERS]
    w_copies = [remote(w_out, w_in.at[i], s_w.at[i], r_w.at[i], (p, f)) for i, p in enumerate(group_at)]
    for c in w_copies:
        c.start()

    for k in range(2):
        swaps[k].wait_recv()

        def add_pair(j, _, k=k):
            columns = pl.ds(pl.multiple_of(j * 128, 128), 128)
            both = terms[half_rows(core, k), columns].astype(F32) + sib[k, :, columns].astype(F32)
            pairs[pl.ds(pl.multiple_of(j * 16, 16), 16), :] = both * CODE
            return 0

        lax.fori_loop(0, 64, add_pair, 0, unroll=4)
        for q in range(4):
            pz = halves[k] * 4 + q
            ahead = lax.rem(pz - z + 8, 8)
            slot = across * 8 + ahead
            for pc in range(2):
                n = k * 8 + q * 2 + pc
                for big in range(8):
                    two = [pairs[pl.ds(big * 128 + q * 4 + pc * 2 + r, 8, stride=16), :] for r in range(2)]
                    whole = jnp.round(jnp.concatenate(two, axis=0)).astype(jnp.int32)
                    out_code[n, big * 16 : big * 16 + 16, :] = whole.astype(jnp.int16)
                copy = remote(
                    out_code.at[n], in_code.at[slot], s_code.at[n], r_code.at[slot], at(core, pz, pc)
                )
                if k == 0:
                    copy.start()
                else:
                    stays = (ahead == 0) & (across == 0) & (core == pc)
                    pl.when(jnp.logical_not(stays))(copy.start)

                    @pl.when(stays)
                    def _(n=n):
                        in_code[0] = out_code[n]

    def code_wait(slot):
        remote(out_code.at[0], in_code.at[slot], s_code.at[0], r_code.at[slot], sibling).wait_recv()

    total = jnp.zeros((128, 128), jnp.int32)
    for d in RING:
        for dx in range(2):
            slot = dx * 8 + d
            if slot:
                code_wait(slot)
            else:
                pl.when(xh != core)(lambda: code_wait(0))
            total = total + in_code[slot].astype(jnp.int32)
    total = total.astype(F32) * (1.0 / CODE)
    for big in range(8):
        for r in range(2):
            summed[pl.ds(big * 16 + r, 8, stride=2), :] = total[big * 16 + r * 8 : big * 16 + r * 8 + 8]

    for c in small[4:]:
        c.wait()
    grad_sum = summed[...]
    moment = old_m[...] + 0.1 * grad_sum
    second = old_s[...] + 0.001 * grad_sum * grad_sum
    update = moment / (1.0 - 0.9**STEP) / (jnp.sqrt(second / (1.0 - 0.999**STEP)) + 1e-08)
    inner = master[...] + drift[...]
    pseudo = master[...] - (inner - 0.8 * (update + 0.025 * inner))
    weighted[...] = weight * pseudo

    def eight(p):
        return pl.ds(pl.multiple_of(p * 8, 8), 8)

    part_copies = [
        remote(weighted.at[eight(p)], part.at[i], s_part.at[i], r_part.at[i], (p, f))
        for i, p in enumerate(group_at)
    ]
    for c in part_copies:
        c.start()
    o_m[...] = moment
    o_s[...] = second
    all_weights = w_out[...]
    for i in range(15):
        w_copies[i].wait_recv()
        all_weights = all_weights + w_in[i]
    own_sum = weighted[eight(g), :]
    for i in range(15):
        part_copies[i].wait_recv()
        own_sum = own_sum + part[i]
    own_mean = own_sum / all_weights

    def nesterov(at_rows, mean_pseudo):
        momentum = 0.9 * mom[at_rows, :] + mean_pseudo
        return master[at_rows, :] - 0.7 * (mean_pseudo + 0.9 * momentum), momentum

    fresh, _ = nesterov(eight(g), own_mean)
    order[...] = fresh
    slice_out[0:4, :] = order[pl.ds(0, 4, stride=2), :]
    slice_out[4:8, :] = order[pl.ds(1, 4, stride=2), :]
    mean[eight(g), :] = own_mean
    slice_copies = []
    for d in RING:
        for dx in (1, 0):
            slot = ((8 - d) % 8) * 2
            to = at((xh + dx) % 2, zs[d], xh)
            n = d * 2 + dx
            where = z * 2 + core
            copy = remote(slice_out, slice_in.at[where], s_slice.at[n], r_slice.at[where], to)
            slice_copies.append(copy)
            if d or dx:
                copy.start()
            else:
                pl.when(xh != core)(copy.start)

                @pl.when(xh == core)
                def _():
                    slice_in[where] = slice_out[...]

    mean_copies = []
    for i, p in enumerate(group_at):
        c = remote(mean.at[eight(g)], mean.at[eight(g)], s_mean.at[i], r_mean.at[i], (p, f))
        c.start()
        mean_copies.append(c)

    def slice_wait(where):
        remote(slice_out, slice_in.at[where], s_slice.at[0], r_slice.at[where], sibling).wait_recv()

    for k in range(8):
        for pc in range(2):
            stays = (xh == core) & (z == k) & (core == pc)
            pl.when(jnp.logical_not(stays))(lambda w=k * 2 + pc: slice_wait(w))
    mine = pl.ds(pl.multiple_of(core * 32, 32), 32)
    flat = slice_in.reshape(128, 128)

    def columns_of(p):
        return pl.ds(pl.multiple_of(p * 512, 512), 512)

    for k in range(2):
        for j in range(4):
            two = [flat[pl.ds((k * 16 + h * 8) * 4 + j, 8, stride=4), :] for h in range(2)]
            o_model[
                pl.ds(pl.multiple_of(core * 32 + k * 16, 16), 16),
                pl.ds(pl.multiple_of(g * 512 + j * 128, 128), 128),
            ] = jnp.concatenate(two, axis=0).astype(BF16)

    def block(p):
        return o_model.at[mine, columns_of(p)]

    block_copies = [
        remote(block(g), block(g), s_block.at[i], r_block.at[i], (p, f)) for i, p in enumerate(group_at)
    ]
    for c in block_copies:
        c.start()
    fwd = [remote(block(g), block(g), s_fwd.at[15], r_fwd.at[15], sibling)]
    fwd[0].start()

    for i, p in enumerate(group_from):
        remote(mean.at[eight(p)], mean.at[eight(p)], s_mean.at[i], r_mean.at[i], sibling).wait_recv()
    everything = pl.ds(0, 128)
    o_master[...], o_mom[...] = nesterov(everything, mean[...])

    for i, p in enumerate(group_from):
        remote(block(p), block(p), s_block.at[i], r_block.at[i], sibling).wait_recv()
        c = remote(block(p), block(p), s_fwd.at[i], r_fwd.at[i], sibling)
        c.start()
        fwd.append(c)

    theirs = pl.ds(pl.multiple_of(other * 32, 32), 32)
    for i, p in enumerate(group_from + [g]):
        there = o_model.at[theirs, columns_of(p)]
        remote(there, there, s_fwd.at[i], r_fwd.at[i], sibling).wait_recv()

    for c in swaps + w_copies + part_copies + mean_copies + block_copies + fwd + slice_copies[:15]:
        c.wait_send()
    pl.when(xh != core)(slice_copies[15].wait_send)
    for n in range(16):
        k, q, pc = n // 8, n // 2 % 4, n % 2
        ahead = lax.rem(halves[k] * 4 + q - z + 8, 8)
        done = remote(out_code.at[n], in_code.at[0], s_code.at[n], r_code.at[0], sibling)
        stays = (ahead == 0) & (across == 0) & (core == pc)
        if k == 0:
            done.wait_send()
        else:
            pl.when(jnp.logical_not(stays))(done.wait_send)


def outer_step(*args):
    hbm = pl.BlockSpec(memory_space=pltpu.HBM)
    vmem = pl.BlockSpec(memory_space=pltpu.VMEM)
    square = pltpu.VMEM((128, 128), F32)
    codes = pltpu.VMEM((128, 128), jnp.int32)
    eight = lambda n: pltpu.VMEM((n, 8, 128), F32)
    dma = pltpu.SemaphoreType.DMA
    out = pltpu.VMEM((128, 128), F32)
    return pl.pallas_call(
        kernel,
        out_shape=(out, out, out, out, pltpu.VMEM((64, 8192), BF16)),
        in_specs=[hbm] * 8 + [pl.BlockSpec(memory_space=pltpu.SMEM)],
        out_specs=(vmem,) * 5,
        scratch_shapes=[
            pltpu.VMEM((64, 8192), BF16), pltpu.VMEM((2, 16, 8192), BF16),
            square, square, square, codes, codes, pltpu.VMEM((1, 2, 32), F32), pltpu.VMEM((1, 2, 32), F32),
            pltpu.VMEM((1024, 128), F32), pltpu.VMEM((16, 128, 128), jnp.int16), pltpu.VMEM((16, 128, 128), jnp.int16),
            square, square, square, square, eight(15), square,
            pltpu.VMEM((8, 128), F32), eight(15), pltpu.VMEM((8, 128), F32), pltpu.VMEM((8, 128), F32), eight(16),
            dma((11,)), dma((2,)), dma((2,)), dma((16,)), dma((16,)), dma((15,)), dma((15,)), dma((15,)), dma((15,)),
            dma((15,)), dma((15,)), dma((16,)), dma((16,)), dma((15,)), dma((15,)), dma((16,)), dma((16,)),
        ],
        compiler_params=pltpu.CompilerParams(
            collective_id=0, has_side_effects=True, vmem_limit_bytes=16 * 1024 * 1024
        ),
        name="outer_step",
    )(*args)


def hand_over(*refs):
    sems = refs[-1]
    copies = [pltpu.make_async_copy(refs[k], refs[5 + k], sems.at[k]) for k in (4, 0, 1, 2, 3)]
    for c in copies:
        c.start()
    for c in copies:
        c.wait()


def on_device(grad_terms, master, inner_drift, momentum, moment_codes, second_codes, moment_scale, second_scale, counts):
    def to_flat(x):
        return x.reshape(2, 64, 128).transpose(1, 0, 2).reshape(128, 128)

    def from_flat(x):
        return x.reshape(64, 2, 128).transpose(1, 0, 2).reshape(2, 8192)

    operands = (
        grad_terms[0, 0], to_flat(master), to_flat(inner_drift), to_flat(momentum),
        to_flat(moment_codes), to_flat(second_codes), moment_scale, second_scale,
    )
    outs = outer_step(*(pltpu.with_memory_space_constraint(x, pltpu.HBM) for x in operands), counts)
    a, b, c, d, model = pl.pallas_call(
        hand_over,
        out_shape=tuple(jax.ShapeDtypeStruct(o.shape, o.dtype) for o in outs),
        in_specs=[pl.BlockSpec(memory_space=pltpu.VMEM)] * 5,
        out_specs=(pl.BlockSpec(memory_space=pltpu.HBM),) * 5,
        scratch_shapes=[pltpu.SemaphoreType.DMA((5,))],
        name="hand_over",
    )(*(pltpu.with_memory_space_constraint(o, pltpu.VMEM) for o in outs))
    return from_flat(a), from_flat(b), from_flat(c)[None], from_flat(d)[None], model


def solution(mesh):
    rows = P("fsdp", None)
    both = P("group", "fsdp", None)
    return jax.shard_map(
        on_device,
        mesh=mesh,
        in_specs=(P("group", "fsdp", None, None), rows, both, rows, both, both, both, both, P("group")),
        out_specs=(rows, rows, both, both, P()),
        check_vma=False,
    )
```

```python
import jax
import jax.numpy as jnp
from jax import lax
from jax.experimental import pallas as pl
from jax.experimental.pallas import tpu as pltpu
from jax.sharding import PartitionSpec as P

BLOCK = 256
STEP = 500
MESH = pl.DeviceIdType.MESH
F32 = jnp.float32
BF16 = jnp.bfloat16
CODE = 27408.0
RING = (4, 3, 5, 2, 6, 1, 7, 0)
PEERS = tuple((dy, dx) for dy in RING for dx in (1, 0))[:15]
PLANE = tuple(sorted(((a, b) for a in range(8) for b in range(8)), key=lambda o: -sum(min(v, 8 - v) for v in o)))
CROSS = (2, 1, 3)


def kernel(
    grad, master_in, drift_in, mom_in, mcode_in, scode_in, mscale_in, sscale_in, counts,
    o_master, o_mom, o_m, o_s, o_model,
    terms, sib, master, drift, mom, mcode, scode, mscale, sscale,
    pairs, out_code, in_code, summed, old_m, old_s, weighted, part, mean, w_out, w_in, order, slice_out, slice_in,
    sorted_rows, s_in, s_sib, r_sib, s_code, r_code, s_w, r_w, s_part, r_part, s_mean, r_mean, s_slice, r_slice,
    s_block, r_block, s_fwd, r_fwd, near, far,
):
    g = lax.axis_index("group")
    f = lax.axis_index("fsdp")
    y, xl = g // 2, g % 2
    xh, z, core = f // 16, (f // 2) % 8, f % 2
    other = 1 - core
    across = (xh + core) % 2
    zs = [lax.rem(z + d, 8) for d in range(8)]
    ys = [lax.rem(y + d, 8) * 2 for d in range(8)]
    back_ys = [lax.rem(y + 8 - d, 8) * 2 for d in range(8)]
    xls = [xl, 1 - xl]

    def at(px, pz, pc):
        return (g, px * 16 + pz * 2 + pc)

    sibling = at(xh, z, other)

    def remote(source, target, send, recv, device):
        return pltpu.make_async_remote_copy(
            source, target, send, recv, device_id=device, device_id_type=MESH
        )

    barrier = pltpu.get_barrier_semaphore()

    def greet(device):
        pl.semaphore_signal(barrier, inc=1, device_id=device, device_id_type=MESH)

    pl.when(core == 1)(lambda: greet(sibling))
    for d in RING:
        greet(at(1 - xh, zs[d], 1))
        if d:
            greet(at(xh, zs[d], 1))
    for dy, dx in PEERS:
        greet((ys[dy] + xls[dx], f + 1 - core))

    loads = [
        pltpu.make_async_copy(grad.at[pl.ds(16 * k, 16)], terms.at[pl.ds(16 * k, 16)], s_in.at[k])
        for k in range(4)
    ]
    small = [
        pltpu.make_async_copy(a, b, s_in.at[4 + k])
        for k, (a, b) in enumerate((
            (mscale_in, mscale), (sscale_in, sscale), (mcode_in, mcode), (scode_in, scode),
            (master_in, master), (drift_in, drift), (mom_in, mom),
        ))
    ]
    for c in loads + small:
        c.start()

    for c in loads:
        c.wait()

    def tell(sem):
        pl.semaphore_signal(sem, inc=1, device_id=sibling, device_id_type=MESH)

    @pl.when(core == 0)
    def _():
        pl.semaphore_wait(barrier, 1)
        tell(near)

    @pl.when(core == 1)
    def _():
        pl.semaphore_wait(near, 1)

    halves = [1 - z // 4, z // 4]

    def half_rows(owner, k):
        return pl.ds(pl.multiple_of(owner * 32 + halves[k] * 16, 16), 16)

    swaps = [
        remote(terms.at[half_rows(other, k)], sib.at[k], s_sib.at[k], r_sib.at[k], sibling) for k in range(2)
    ]
    for c in swaps:
        c.start()

    for c in small[:4]:
        c.wait()
    weight = counts[0].astype(F32)
    w_out[...] = jnp.full((8, 128), weight, F32)
    rows = lax.broadcasted_iota(jnp.int32, (128, 32), 0)
    hit = lax.broadcasted_iota(jnp.int32, (128, 32), 1) == rows // 4

    def scale_of(ref):
        both = jnp.where(rows % 2 == 0, ref[0, 0:1, :], ref[0, 1:2, :])
        return jnp.sum(jnp.where(hit, both, 0.0), axis=1, keepdims=True)

    signed = (mcode[...].astype(F32) - 127.5) / 127.5
    old_m[...] = 0.9 * (signed * signed * signed * scale_of(mscale))
    unsigned = (scode[...].astype(F32) + 16.0) / 271.0
    old_s[...] = 0.999 * (unsigned * unsigned * scale_of(sscale))
    for k in range(2):
        swaps[k].wait_recv()

        def add_pair(j, _, k=k):
            columns = pl.ds(pl.multiple_of(j * 128, 128), 128)
            both = terms[half_rows(core, k), columns].astype(F32) + sib[k, :, columns].astype(F32)
            pairs[pl.ds(pl.multiple_of(j * 16, 16), 16), :] = both * CODE
            return 0

        lax.fori_loop(0, 64, add_pair, 0, unroll=4)
        if k == 0:

            @pl.when(core == 1)
            def _():
                pl.semaphore_wait(barrier, 60)
                tell(far)

            @pl.when(core == 0)
            def _():
                pl.semaphore_wait(far, 1)

        for q in range(4):
            pz = halves[k] * 4 + q
            ahead = lax.rem(pz - z + 8, 8)
            slot = across * 8 + ahead
            for pc in range(2):
                n = k * 8 + q * 2 + pc
                for big in range(8):
                    two = [pairs[pl.ds(big * 128 + q * 4 + pc * 2 + r, 8, stride=16), :] for r in range(2)]
                    whole = jnp.round(jnp.concatenate(two, axis=0)).astype(jnp.int32)
                    out_code[n, big * 16 : big * 16 + 16, :] = whole.astype(jnp.int16)
                copy = remote(
                    out_code.at[n], in_code.at[slot], s_code.at[n], r_code.at[slot], at(core, pz, pc)
                )
                if k == 0:
                    copy.start()
                else:
                    stays = (ahead == 0) & (across == 0) & (core == pc)
                    pl.when(jnp.logical_not(stays))(copy.start)

                    @pl.when(stays)
                    def _(n=n):
                        in_code[0] = out_code[n]

    group_at = [(ys[dy] + xls[dx], xls[dx] * 8 + ys[dy] // 2) for dy, dx in PEERS]
    group_from = [xls[dx] * 8 + back_ys[dy] // 2 for dy, dx in PEERS]
    own_eight = xl * 8 + y
    w_copies = [remote(w_out, w_in.at[i], s_w.at[i], r_w.at[i], (p, f)) for i, (p, _) in enumerate(group_at)]
    for c in w_copies:
        c.start()

    def code_wait(slot):
        remote(out_code.at[0], in_code.at[slot], s_code.at[0], r_code.at[slot], sibling).wait_recv()

    total = jnp.zeros((128, 128), jnp.int32)
    for d in RING:
        for dx in range(2):
            slot = dx * 8 + d
            if slot:
                code_wait(slot)
            else:
                pl.when(xh != core)(lambda: code_wait(0))
            total = total + in_code[slot].astype(jnp.int32)
    total = total.astype(F32) * (1.0 / CODE)
    for big in range(8):
        for r in range(2):
            summed[pl.ds(big * 16 + r, 8, stride=2), :] = total[big * 16 + r * 8 : big * 16 + r * 8 + 8]

    for c in small[4:]:
        c.wait()
    grad_sum = summed[...]
    moment = old_m[...] + 0.1 * grad_sum
    second = old_s[...] + 0.001 * grad_sum * grad_sum
    update = moment / (1.0 - 0.9**STEP) / (jnp.sqrt(second / (1.0 - 0.999**STEP)) + 1e-08)
    inner = master[...] + drift[...]
    pseudo = master[...] - (inner - 0.8 * (update + 0.025 * inner))
    weighted[...] = weight * pseudo

    def eight(p):
        return pl.ds(pl.multiple_of(p * 8, 8), 8)

    part_copies = [
        remote(weighted.at[eight(e)], part.at[i], s_part.at[i], r_part.at[i], (p, f))
        for i, (p, e) in enumerate(group_at)
    ]
    for c in part_copies:
        c.start()
    o_m[...] = moment
    o_s[...] = second
    all_weights = w_out[...]
    for i in range(15):
        w_copies[i].wait_recv()
        all_weights = all_weights + w_in[i]
    own_sum = weighted[eight(own_eight), :]
    for i in range(15):
        part_copies[i].wait_recv()
        own_sum = own_sum + part[i]
    own_mean = own_sum / all_weights

    def nesterov(at_rows, mean_pseudo):
        momentum = 0.9 * mom[at_rows, :] + mean_pseudo
        return master[at_rows, :] - 0.7 * (mean_pseudo + 0.9 * momentum), momentum

    fresh, _ = nesterov(eight(own_eight), own_mean)
    order[...] = fresh
    two = [order[pl.ds(r, 4, stride=2), :] for r in range(2)]
    slice_out[0] = jnp.concatenate(two, axis=0).astype(BF16)
    mean[eight(own_eight), :] = own_mean
    half = z // 4
    where = y * 8 + lax.rem(z, 4) * 2 + core
    slice_copies = []
    for n, (dy, dz) in enumerate(PLANE):
        to = (ys[dy] + xl, xh * 16 + zs[dz] * 2 + half)
        copy = remote(slice_out.at[0], slice_in.at[where], s_slice.at[n], r_slice.at[where], to)
        slice_copies.append(copy)
        if n < 63:
            copy.start()
        else:
            pl.when(half != core)(copy.start)
            keep = pltpu.make_async_copy(slice_out.at[0], slice_in.at[where], r_slice.at[where])
            pl.when(half == core)(keep.start)

    mean_copies = []
    mine = mean.at[eight(own_eight)]
    for i, (p, _) in enumerate(group_at):
        c = remote(mine, mine, s_mean.at[i], r_mean.at[i], (p, f))
        c.start()
        mean_copies.append(c)

    x = xh * 2 + xl
    xs = [lax.rem(x + d, 4) for d in range(4)]

    def block(source_x, source_core, d):
        row = (source_x // 2 * 2 + source_core) * 16
        column = (lax.rem(source_x, 2) * 8 + ys[d] // 2) * 512
        return o_model.at[pl.ds(pl.multiple_of(row, 16), 16), pl.ds(pl.multiple_of(column, 512), 512)]

    sends = []
    for n, d in enumerate(reversed(RING)):
        from_y = ys[d] // 2
        for k in range(8):
            slot = from_y * 8 + k
            remote(slice_out.at[0], slice_in.at[slot], s_slice.at[0], r_slice.at[slot], sibling).wait_recv()
        wide = slice_in[pl.ds(pl.multiple_of(from_y * 8, 8), 8)].astype(F32)
        sorted_rows[...] = wide.reshape(64, 128)
        piece = block(x, core, d)
        for j in range(4):
            two = [sorted_rows[pl.ds(h * 32 + j, 8, stride=4), :] for h in range(2)]
            piece[:, j * 128 : j * 128 + 128] = jnp.concatenate(two, axis=0).astype(BF16)
        for dx in CROSS:
            to = (y * 2 + lax.rem(xs[dx], 2), xs[dx] // 2 * 16 + z * 2 + core)
            sends.append(remote(piece, piece, s_block.at[dx * 8 + n], r_block.at[dx * 8 + n], to))
            sends[-1].start()
        sends.append(remote(piece, piece, s_fwd.at[n], r_fwd.at[n], sibling))
        sends[-1].start()

    for i, e in enumerate(group_from):
        remote(mean.at[eight(e)], mean.at[eight(e)], s_mean.at[i], r_mean.at[i], sibling).wait_recv()
    everything = pl.ds(0, 128)
    o_master[...], o_mom[...] = nesterov(everything, mean[...])

    for c in swaps + w_copies + part_copies + mean_copies + slice_copies[:63]:
        c.wait_send()
    pl.when(half != core)(slice_copies[63].wait_send)
    for n in range(16):
        k, q, pc = n // 8, n // 2 % 4, n % 2
        ahead = lax.rem(halves[k] * 4 + q - z + 8, 8)
        done = remote(out_code.at[n], in_code.at[0], s_code.at[n], r_code.at[0], sibling)
        stays = (ahead == 0) & (across == 0) & (core == pc)
        if k == 0:
            done.wait_send()
        else:
            pl.when(jnp.logical_not(stays))(done.wait_send)

    for n, d in enumerate(reversed(RING)):
        for dx in CROSS:
            piece = block(xs[4 - dx], core, d)
            at_n = dx * 8 + n
            remote(piece, piece, s_block.at[at_n], r_block.at[at_n], sibling).wait_recv()
            sends.append(remote(piece, piece, s_fwd.at[at_n], r_fwd.at[at_n], sibling))
            sends[-1].start()
    for n, d in enumerate(reversed(RING)):
        for dx in (0,) + CROSS:
            piece = block(xs[(4 - dx) % 4], other, d)
            at_n = dx * 8 + n
            remote(piece, piece, s_fwd.at[at_n], r_fwd.at[at_n], sibling).wait_recv()
    for c in sends:
        c.wait_send()


def outer_step(*args):
    hbm = pl.BlockSpec(memory_space=pltpu.HBM)
    vmem = pl.BlockSpec(memory_space=pltpu.VMEM)
    square = pltpu.VMEM((128, 128), F32)
    codes = pltpu.VMEM((128, 128), jnp.int32)
    eight = lambda n: pltpu.VMEM((n, 8, 128), F32)
    dma = pltpu.SemaphoreType.DMA
    out = pltpu.VMEM((128, 128), F32)
    return pl.pallas_call(
        kernel,
        out_shape=(out, out, out, out, pltpu.VMEM((64, 8192), BF16)),
        in_specs=[hbm] * 8 + [pl.BlockSpec(memory_space=pltpu.SMEM)],
        out_specs=(vmem,) * 5,
        scratch_shapes=[
            pltpu.VMEM((64, 8192), BF16), pltpu.VMEM((2, 16, 8192), BF16),
            square, square, square, codes, codes, pltpu.VMEM((1, 2, 32), F32), pltpu.VMEM((1, 2, 32), F32),
            pltpu.VMEM((1024, 128), F32), pltpu.VMEM((16, 128, 128), jnp.int16), pltpu.VMEM((16, 128, 128), jnp.int16),
            square, square, square, square, eight(15), square,
            pltpu.VMEM((8, 128), F32), eight(15), pltpu.VMEM((8, 128), F32),
            pltpu.VMEM((1, 8, 128), BF16), pltpu.VMEM((64, 8, 128), BF16), pltpu.VMEM((64, 128), F32),
            dma((11,)), dma((2,)), dma((2,)), dma((16,)), dma((16,)), dma((15,)), dma((15,)), dma((15,)), dma((15,)),
            dma((15,)), dma((15,)), dma((64,)), dma((64,)), dma((32,)), dma((32,)), dma((32,)), dma((32,)),
            pltpu.SemaphoreType.REGULAR, pltpu.SemaphoreType.REGULAR,
        ],
        compiler_params=pltpu.CompilerParams(
            collective_id=0, has_side_effects=True, vmem_limit_bytes=16 * 1024 * 1024
        ),
        name="outer_step",
    )(*args)


def hand_over(*refs):
    sems = refs[-1]
    copies = [pltpu.make_async_copy(refs[k], refs[5 + k], sems.at[k]) for k in (4, 0, 1, 2, 3)]
    for c in copies:
        c.start()
    for c in copies:
        c.wait()


def on_device(grad_terms, master, inner_drift, momentum, moment_codes, second_codes, moment_scale, second_scale, counts):
    def to_flat(x):
        return x.reshape(2, 64, 128).transpose(1, 0, 2).reshape(128, 128)

    def from_flat(x):
        return x.reshape(64, 2, 128).transpose(1, 0, 2).reshape(2, 8192)

    operands = (
        grad_terms[0, 0], to_flat(master), to_flat(inner_drift), to_flat(momentum),
        to_flat(moment_codes), to_flat(second_codes), moment_scale, second_scale,
    )
    outs = outer_step(*(pltpu.with_memory_space_constraint(x, pltpu.HBM) for x in operands), counts)
    a, b, c, d, model = pl.pallas_call(
        hand_over,
        out_shape=tuple(jax.ShapeDtypeStruct(o.shape, o.dtype) for o in outs),
        in_specs=[pl.BlockSpec(memory_space=pltpu.VMEM)] * 5,
        out_specs=(pl.BlockSpec(memory_space=pltpu.HBM),) * 5,
        scratch_shapes=[pltpu.SemaphoreType.DMA((5,))],
        name="hand_over",
    )(*(pltpu.with_memory_space_constraint(o, pltpu.VMEM) for o in outs))
    return from_flat(a), from_flat(b), from_flat(c)[None], from_flat(d)[None], model


def solution(mesh):
    rows = P("fsdp", None)
    both = P("group", "fsdp", None)
    return jax.shard_map(
        on_device,
        mesh=mesh,
        in_specs=(P("group", "fsdp", None, None), rows, both, rows, both, both, both, both, P("group")),
        out_specs=(rows, rows, both, both, P()),
        check_vma=False,
    )
```

```python
import jax
import jax.numpy as jnp
from jax import lax
from jax.experimental import pallas as pl
from jax.experimental.pallas import tpu as pltpu
from jax.sharding import PartitionSpec as P

BLOCK = 256
STEP = 500
MESH = pl.DeviceIdType.MESH
F32 = jnp.float32
BF16 = jnp.bfloat16
CODE = 27408.0
RING = (4, 3, 5, 2, 6, 1, 7, 0)
PEERS = tuple((dy, dx) for dy in RING for dx in (1, 0))[:15]
PLANE = tuple(sorted(((a, b) for a in range(8) for b in range(8)), key=lambda o: -sum(min(v, 8 - v) for v in o)))
CROSS = (2, 1, 3)


def kernel(
    grad, master_in, drift_in, mom_in, mcode_in, scode_in, mscale_in, sscale_in, counts,
    o_master, o_mom, o_m, o_s, o_model,
    terms, sib, master, drift, mom, mcode, scode, mscale, sscale,
    wide, by_owner, cross_code, out_code, x_code, in_code, summed, old_m, old_s, weighted, part, mean, w_out, w_in, order, slice_out, slice_in,
    sorted_rows, s_in, s_sib, r_sib, s_code, r_code, s_x, r_x, s_w, r_w, s_part, r_part, s_mean, r_mean, s_slice, r_slice,
    s_block, r_block, s_fwd, r_fwd, near, far,
):
    g = lax.axis_index("group")
    f = lax.axis_index("fsdp")
    y, xl = g // 2, g % 2
    xh, z, core = f // 16, (f // 2) % 8, f % 2
    other = 1 - core
    zs = [lax.rem(z + d, 8) for d in range(8)]
    ys = [lax.rem(y + d, 8) * 2 for d in range(8)]
    back_ys = [lax.rem(y + 8 - d, 8) * 2 for d in range(8)]
    xls = [xl, 1 - xl]

    def at(px, pz, pc):
        return (g, px * 16 + pz * 2 + pc)

    sibling = at(xh, z, other)

    def remote(source, target, send, recv, device):
        return pltpu.make_async_remote_copy(
            source, target, send, recv, device_id=device, device_id_type=MESH
        )

    barrier = pltpu.get_barrier_semaphore()

    def greet(device):
        pl.semaphore_signal(barrier, inc=1, device_id=device, device_id_type=MESH)

    pl.when(core == 1)(lambda: greet(sibling))
    for d in RING:
        greet(at(xh, zs[d], 1) if d else at(1 - xh, z, 1))
    for dy, dx in PEERS:
        greet((ys[dy] + xls[dx], f + 1 - core))

    z_half = z // 4
    tiles = [px * 2 + pz for px in (1 - xh, xh) for pz in (1 - z_half, z_half)]

    def sixteen(t):
        return pl.ds(pl.multiple_of(t * 16, 16), 16)

    loads = [
        pltpu.make_async_copy(grad.at[sixteen(t)], terms.at[sixteen(t)], s_in.at[k]) for k, t in enumerate(tiles)
    ]
    small = [
        pltpu.make_async_copy(a, b, s_in.at[4 + k])
        for k, (a, b) in enumerate((
            (mscale_in, mscale), (sscale_in, sscale), (mcode_in, mcode), (scode_in, scode),
            (master_in, master), (drift_in, drift), (mom_in, mom),
        ))
    ]
    for c in loads + small:
        c.start()

    def regroup(k):
        loads[k].wait()

        def widen(j, _):
            columns = pl.ds(pl.multiple_of(j * 128, 128), 128)
            wide[pl.ds(pl.multiple_of(j * 16, 16), 16), :] = terms[sixteen(tiles[k]), columns].astype(F32)
            return 0

        lax.fori_loop(0, 64, widen, 0, unroll=4)
        for q in range(4):
            for pc in range(2):
                for big in range(8):
                    two = [wide[pl.ds(big * 128 + q * 4 + pc * 2 + r, 8, stride=16), :] for r in range(2)]
                    by_owner[pc, tiles[k] * 4 + q, big * 16 : big * 16 + 16, :] = jnp.concatenate(two, axis=0).astype(
                        BF16
                    )

    def four(t):
        return pl.ds(t * 4, 4)

    swaps = [
        remote(by_owner.at[other, four(t)], sib.at[four(t)], s_sib.at[k], r_sib.at[k], sibling)
        for k, t in enumerate(tiles)
    ]
    regroup(0)

    def tell(sem):
        pl.semaphore_signal(sem, inc=1, device_id=sibling, device_id_type=MESH)

    @pl.when(core == 0)
    def _():
        pl.semaphore_wait(barrier, 1)
        tell(near)

    @pl.when(core == 1)
    def _():
        pl.semaphore_wait(near, 1)

    swaps[0].start()
    for k in range(1, 4):
        regroup(k)
        swaps[k].start()

    for c in small[:4]:
        c.wait()
    weight = counts[0].astype(F32)
    w_out[...] = jnp.full((8, 128), weight, F32)
    rows = lax.broadcasted_iota(jnp.int32, (128, 32), 0)
    hit = lax.broadcasted_iota(jnp.int32, (128, 32), 1) == rows // 4

    def scale_of(ref):
        both = jnp.where(rows % 2 == 0, ref[0, 0:1, :], ref[0, 1:2, :])
        return jnp.sum(jnp.where(hit, both, 0.0), axis=1, keepdims=True)

    signed = (mcode[...].astype(F32) - 127.5) / 127.5
    old_m[...] = 0.9 * (signed * signed * signed * scale_of(mscale))
    unsigned = (scode[...].astype(F32) + 16.0) / 271.0
    old_s[...] = 0.999 * (unsigned * unsigned * scale_of(sscale))

    @pl.when(core == 1)
    def _():
        pl.semaphore_wait(barrier, 46)
        tell(far)

    @pl.when(core == 0)
    def _():
        pl.semaphore_wait(far, 1)

    def pair(chip):
        return by_owner[core, chip].astype(F32) + sib[chip].astype(F32)

    def to_codes(values):
        return jnp.round(values).astype(jnp.int32).astype(jnp.int16)

    crossing = []
    for k in range(2):
        swaps[k].wait_recv()
        for q in range(4):
            pz = lax.rem(tiles[k], 2) * 4 + q
            cross_code[pz] = to_codes(pair(tiles[k] * 4 + q) * CODE)
            c = remote(cross_code.at[pz], x_code.at[pz], s_x.at[k * 4 + q], r_x.at[pz], at(1 - xh, z, core))
            c.start()
            crossing.append(c)

    along = []
    for k in range(2):
        swaps[2 + k].wait_recv()
        for q in range(4):
            pz = lax.rem(tiles[2 + k], 2) * 4 + q
            mine = pair(tiles[2 + k] * 4 + q) * CODE
            remote(x_code.at[pz], x_code.at[pz], s_x.at[0], r_x.at[pz], sibling).wait_recv()
            both = to_codes(0.5 * (mine + x_code[pz].astype(F32)))
            c = remote(out_code.at[pz], in_code.at[z], s_code.at[k * 4 + q], r_code.at[z], at(xh, pz, core))
            along.append(c)
            if k == 0:
                out_code[pz] = both
                c.start()
            else:
                @pl.when(lax.rem(z, 4) == q)
                def _(both=both):
                    in_code[z] = both

                @pl.when(lax.rem(z, 4) != q)
                def _(both=both, c=c, pz=pz):
                    out_code[pz] = both
                    c.start()

    group_at = [(ys[dy] + xls[dx], xls[dx] * 8 + ys[dy] // 2) for dy, dx in PEERS]
    group_from = [xls[dx] * 8 + back_ys[dy] // 2 for dy, dx in PEERS]
    own_eight = xl * 8 + y
    w_copies = [remote(w_out, w_in.at[i], s_w.at[i], r_w.at[i], (p, f)) for i, (p, _) in enumerate(group_at)]
    for c in w_copies:
        c.start()

    total = jnp.zeros((128, 128), jnp.int32)
    for slot in range(8):
        c = remote(out_code.at[slot], in_code.at[slot], s_code.at[0], r_code.at[slot], sibling)
        pl.when(slot != z)(c.wait_recv)
        total = total + in_code[slot].astype(jnp.int32)
    total = total.astype(F32) * (2.0 / CODE)
    for big in range(8):
        for r in range(2):
            summed[pl.ds(big * 16 + r, 8, stride=2), :] = total[big * 16 + r * 8 : big * 16 + r * 8 + 8]

    for c in small[4:]:
        c.wait()
    grad_sum = summed[...]
    moment = old_m[...] + 0.1 * grad_sum
    second = old_s[...] + 0.001 * grad_sum * grad_sum
    update = moment / (1.0 - 0.9**STEP) / (jnp.sqrt(second / (1.0 - 0.999**STEP)) + 1e-08)
    inner = master[...] + drift[...]
    pseudo = master[...] - (inner - 0.8 * (update + 0.025 * inner))
    weighted[...] = weight * pseudo

    def eight(p):
        return pl.ds(pl.multiple_of(p * 8, 8), 8)

    part_copies = [
        remote(weighted.at[eight(e)], part.at[i], s_part.at[i], r_part.at[i], (p, f))
        for i, (p, e) in enumerate(group_at)
    ]
    for c in part_copies:
        c.start()
    o_m[...] = moment
    o_s[...] = second
    all_weights = w_out[...]
    for i in range(15):
        w_copies[i].wait_recv()
        all_weights = all_weights + w_in[i]
    own_sum = weighted[eight(own_eight), :]
    for i in range(15):
        part_copies[i].wait_recv()
        own_sum = own_sum + part[i]
    own_mean = own_sum / all_weights

    def nesterov(at_rows, mean_pseudo):
        momentum = 0.9 * mom[at_rows, :] + mean_pseudo
        return master[at_rows, :] - 0.7 * (mean_pseudo + 0.9 * momentum), momentum

    fresh, _ = nesterov(eight(own_eight), own_mean)
    order[...] = fresh
    two = [order[pl.ds(r, 4, stride=2), :] for r in range(2)]
    slice_out[0] = jnp.concatenate(two, axis=0).astype(BF16)
    mean[eight(own_eight), :] = own_mean
    where = y * 8 + lax.rem(z, 4) * 2 + core
    slice_copies = []
    for n, (dy, dz) in enumerate(PLANE):
        to = (ys[dy] + xl, xh * 16 + zs[dz] * 2 + z_half)
        copy = remote(slice_out.at[0], slice_in.at[where], s_slice.at[n], r_slice.at[where], to)
        slice_copies.append(copy)
        if n < 63:
            copy.start()
        else:
            pl.when(z_half != core)(copy.start)
            keep = pltpu.make_async_copy(slice_out.at[0], slice_in.at[where], r_slice.at[where])
            pl.when(z_half == core)(keep.start)

    mean_copies = []
    own_rows = mean.at[eight(own_eight)]
    for i, (p, _) in enumerate(group_at):
        c = remote(own_rows, own_rows, s_mean.at[i], r_mean.at[i], (p, f))
        c.start()
        mean_copies.append(c)

    x = xh * 2 + xl
    xs = [lax.rem(x + d, 4) for d in range(4)]

    def block(source_x, source_core, d):
        row = (source_x // 2 * 2 + source_core) * 16
        column = (lax.rem(source_x, 2) * 8 + ys[d] // 2) * 512
        return o_model.at[pl.ds(pl.multiple_of(row, 16), 16), pl.ds(pl.multiple_of(column, 512), 512)]

    sends = []
    for n, d in enumerate(reversed(RING)):
        from_y = ys[d] // 2
        for k in range(8):
            slot = from_y * 8 + k
            remote(slice_out.at[0], slice_in.at[slot], s_slice.at[0], r_slice.at[slot], sibling).wait_recv()
        arrived = slice_in[pl.ds(pl.multiple_of(from_y * 8, 8), 8)].astype(F32)
        sorted_rows[...] = arrived.reshape(64, 128)
        piece = block(x, core, d)
        for j in range(4):
            two = [sorted_rows[pl.ds(h * 32 + j, 8, stride=4), :] for h in range(2)]
            piece[:, j * 128 : j * 128 + 128] = jnp.concatenate(two, axis=0).astype(BF16)
        for dx in CROSS:
            to = (y * 2 + lax.rem(xs[dx], 2), xs[dx] // 2 * 16 + z * 2 + core)
            sends.append(remote(piece, piece, s_block.at[dx * 8 + n], r_block.at[dx * 8 + n], to))
            sends[-1].start()
        sends.append(remote(piece, piece, s_fwd.at[n], r_fwd.at[n], sibling))
        sends[-1].start()

    for i, e in enumerate(group_from):
        remote(mean.at[eight(e)], mean.at[eight(e)], s_mean.at[i], r_mean.at[i], sibling).wait_recv()
    everything = pl.ds(0, 128)
    o_master[...], o_mom[...] = nesterov(everything, mean[...])

    for c in swaps + crossing + w_copies + part_copies + mean_copies + slice_copies[:63]:
        c.wait_send()
    pl.when(z_half != core)(slice_copies[63].wait_send)
    for q in range(4):
        along[q].wait_send()
        pl.when(lax.rem(z, 4) != q)(along[4 + q].wait_send)

    for n, d in enumerate(reversed(RING)):
        for dx in CROSS:
            piece = block(xs[4 - dx], core, d)
            at_n = dx * 8 + n
            remote(piece, piece, s_block.at[at_n], r_block.at[at_n], sibling).wait_recv()
            sends.append(remote(piece, piece, s_fwd.at[at_n], r_fwd.at[at_n], sibling))
            sends[-1].start()
    for n, d in enumerate(reversed(RING)):
        for dx in (0,) + CROSS:
            piece = block(xs[(4 - dx) % 4], other, d)
            at_n = dx * 8 + n
            remote(piece, piece, s_fwd.at[at_n], r_fwd.at[at_n], sibling).wait_recv()
    for c in sends:
        c.wait_send()


def outer_step(*args):
    hbm = pl.BlockSpec(memory_space=pltpu.HBM)
    vmem = pl.BlockSpec(memory_space=pltpu.VMEM)
    square = pltpu.VMEM((128, 128), F32)
    codes = pltpu.VMEM((128, 128), jnp.int32)
    codes16 = pltpu.VMEM((8, 128, 128), jnp.int16)
    eight = lambda n: pltpu.VMEM((n, 8, 128), F32)
    dma = pltpu.SemaphoreType.DMA
    out = pltpu.VMEM((128, 128), F32)
    return pl.pallas_call(
        kernel,
        out_shape=(out, out, out, out, pltpu.VMEM((64, 8192), BF16)),
        in_specs=[hbm] * 8 + [pl.BlockSpec(memory_space=pltpu.SMEM)],
        out_specs=(vmem,) * 5,
        scratch_shapes=[
            pltpu.VMEM((64, 8192), BF16), pltpu.VMEM((16, 128, 128), BF16),
            square, square, square, codes, codes, pltpu.VMEM((1, 2, 32), F32), pltpu.VMEM((1, 2, 32), F32),
            pltpu.VMEM((1024, 128), F32), pltpu.VMEM((2, 16, 128, 128), BF16), codes16, codes16, codes16, codes16,
            square, square, square, square, eight(15), square,
            pltpu.VMEM((8, 128), F32), eight(15), pltpu.VMEM((8, 128), F32),
            pltpu.VMEM((1, 8, 128), BF16), pltpu.VMEM((64, 8, 128), BF16), pltpu.VMEM((64, 128), F32),
            dma((11,)), dma((4,)), dma((4,)), dma((8,)), dma((8,)), dma((8,)), dma((8,)), dma((15,)), dma((15,)), dma((15,)),
            dma((15,)), dma((15,)), dma((15,)), dma((64,)), dma((64,)), dma((32,)), dma((32,)), dma((32,)), dma((32,)),
            pltpu.SemaphoreType.REGULAR, pltpu.SemaphoreType.REGULAR,
        ],
        compiler_params=pltpu.CompilerParams(
            collective_id=0, has_side_effects=True, vmem_limit_bytes=16 * 1024 * 1024
        ),
        name="outer_step",
    )(*args)


def hand_over(*refs):
    sems = refs[-1]
    copies = [pltpu.make_async_copy(refs[k], refs[5 + k], sems.at[k]) for k in (4, 0, 1, 2, 3)]
    for c in copies:
        c.start()
    for c in copies:
        c.wait()


def on_device(grad_terms, master, inner_drift, momentum, moment_codes, second_codes, moment_scale, second_scale, counts):
    def to_flat(x):
        return x.reshape(2, 64, 128).transpose(1, 0, 2).reshape(128, 128)

    def from_flat(x):
        return x.reshape(64, 2, 128).transpose(1, 0, 2).reshape(2, 8192)

    operands = (
        grad_terms[0, 0], to_flat(master), to_flat(inner_drift), to_flat(momentum),
        to_flat(moment_codes), to_flat(second_codes), moment_scale, second_scale,
    )
    outs = outer_step(*(pltpu.with_memory_space_constraint(x, pltpu.HBM) for x in operands), counts)
    a, b, c, d, model = pl.pallas_call(
        hand_over,
        out_shape=tuple(jax.ShapeDtypeStruct(o.shape, o.dtype) for o in outs),
        in_specs=[pl.BlockSpec(memory_space=pltpu.VMEM)] * 5,
        out_specs=(pl.BlockSpec(memory_space=pltpu.HBM),) * 5,
        scratch_shapes=[pltpu.SemaphoreType.DMA((5,))],
        name="hand_over",
    )(*(pltpu.with_memory_space_constraint(o, pltpu.VMEM) for o in outs))
    return from_flat(a), from_flat(b), from_flat(c)[None], from_flat(d)[None], model


def solution(mesh):
    rows = P("fsdp", None)
    both = P("group", "fsdp", None)
    return jax.shard_map(
        on_device,
        mesh=mesh,
        in_specs=(P("group", "fsdp", None, None), rows, both, rows, both, both, both, both, P("group")),
        out_specs=(rows, rows, both, both, P()),
        check_vma=False,
    )
```

```python
import jax
import jax.numpy as jnp
from jax import lax
from jax.experimental import pallas as pl
from jax.experimental.pallas import tpu as pltpu
from jax.sharding import PartitionSpec as P

BLOCK = 256
STEP = 500
MESH = pl.DeviceIdType.MESH
F32 = jnp.float32
BF16 = jnp.bfloat16
CODE = 27408.0
RING = (4, 3, 5, 2, 6, 1, 7, 0)
PEERS = tuple((dy, dx) for dy in RING for dx in (1, 0))[:15]
PLANE = tuple((dy, dz) for dy in reversed(RING) for dz in RING if dy or dz)
CROSS = (2, 1, 3)


def kernel(
    grad, master_in, drift_in, mom_in, mcode_in, scode_in, mscale_in, sscale_in, counts,
    o_master, o_mom, o_m, o_s, o_model,
    terms, sib, master, drift, mom, mcode, scode, mscale, sscale,
    wide, by_owner, cross_code, out_code, x_code, in_code, summed, old_m, old_s, weighted, part, mean, w_out, w_in, order, slice_out, slice_in,
    sorted_rows, s_in, s_sib, r_sib, s_code, r_code, s_x, r_x, s_w, r_w, s_part, r_part, s_mean, r_mean, s_slice, r_slice,
    s_block, r_block, s_fwd, r_fwd, near, far,
):
    g = lax.axis_index("group")
    f = lax.axis_index("fsdp")
    y, xl = g // 2, g % 2
    xh, z, core = f // 16, (f // 2) % 8, f % 2
    other = 1 - core
    zs = [lax.rem(z + d, 8) for d in range(8)]
    ys = [lax.rem(y + d, 8) * 2 for d in range(8)]
    back_ys = [lax.rem(y + 8 - d, 8) * 2 for d in range(8)]
    xls = [xl, 1 - xl]

    def at(px, pz, pc):
        return (g, px * 16 + pz * 2 + pc)

    sibling = at(xh, z, other)

    def remote(source, target, send, recv, device):
        return pltpu.make_async_remote_copy(
            source, target, send, recv, device_id=device, device_id_type=MESH
        )

    barrier = pltpu.get_barrier_semaphore()

    def greet(device):
        pl.semaphore_signal(barrier, inc=1, device_id=device, device_id_type=MESH)

    across_x = at(1 - xh, z, core)
    greet(at(1 - xh, z, 0))
    pl.when(core == 1)(lambda: greet(sibling))
    z_half = z // 4
    tiles = [px * 2 + pz for px in (1 - xh, xh) for pz in (1 - z_half, z_half)]

    def sixteen(t):
        return pl.ds(pl.multiple_of(t * 16, 16), 16)

    loads = [
        pltpu.make_async_copy(grad.at[sixteen(t)], terms.at[sixteen(t)], s_in.at[k]) for k, t in enumerate(tiles)
    ]
    small = [
        pltpu.make_async_copy(a, b, s_in.at[4 + k])
        for k, (a, b) in enumerate((
            (mscale_in, mscale), (sscale_in, sscale), (mcode_in, mcode), (scode_in, scode),
            (master_in, master), (drift_in, drift), (mom_in, mom),
        ))
    ]
    for c in loads + small:
        c.start()

    def regroup(k):
        loads[k].wait()

        def widen(j, _):
            columns = pl.ds(pl.multiple_of(j * 128, 128), 128)
            wide[pl.ds(pl.multiple_of(j * 16, 16), 16), :] = terms[sixteen(tiles[k]), columns].astype(F32)
            return 0

        lax.fori_loop(0, 64, widen, 0, unroll=4)
        for q in range(4):
            for pc in range(2):
                for big in range(8):
                    two = [wide[pl.ds(big * 128 + q * 4 + pc * 2 + r, 8, stride=16), :] for r in range(2)]
                    by_owner[pc, tiles[k] * 4 + q, big * 16 : big * 16 + 16, :] = jnp.concatenate(two, axis=0).astype(
                        BF16
                    )

    for k in range(4):
        regroup(k)

    chips = [(1 - xh) * 8 + zs[d] for d in RING] + [xh * 8 + zs[d] for d in RING]
    swaps = [
        remote(by_owner.at[other, chip], sib.at[k], s_sib.at[k], r_sib.at[k], sibling)
        for k, chip in enumerate(chips)
    ]

    def tell(sem):
        pl.semaphore_signal(sem, inc=1, device_id=sibling, device_id_type=MESH)

    @pl.when(core == 0)
    def _():
        pl.semaphore_wait(barrier, 3)
        tell(near)

    @pl.when(core == 1)
    def _():
        pl.semaphore_wait(near, 1)

    for c in swaps:
        c.start()
    for d in RING[:7]:
        greet(at(xh, zs[d], 1))
    for dy, dx in PEERS:
        greet((ys[dy] + xls[dx], f + 1 - core))

    def pair(k):
        swaps[k].wait_recv()
        return by_owner[core, chips[k]].astype(F32) + sib[k].astype(F32)

    def to_codes(values):
        return jnp.round(values).astype(jnp.int32).astype(jnp.int16)

    crossing = []
    for k, d in enumerate(RING):
        cross_code[d] = to_codes(pair(k) * CODE)
        c = remote(cross_code.at[d], x_code.at[d], s_x.at[d], r_x.at[d], across_x)
        c.start()
        crossing.append(c)

    for c in small[:4]:
        c.wait()
    weight = counts[0].astype(F32)
    w_out[...] = jnp.full((8, 128), weight, F32)
    rows = lax.broadcasted_iota(jnp.int32, (128, 32), 0)
    hit = lax.broadcasted_iota(jnp.int32, (128, 32), 1) == rows // 4

    def scale_of(ref):
        both = jnp.where(rows % 2 == 0, ref[0, 0:1, :], ref[0, 1:2, :])
        return jnp.sum(jnp.where(hit, both, 0.0), axis=1, keepdims=True)

    signed = (mcode[...].astype(F32) - 127.5) / 127.5
    old_m[...] = 0.9 * (signed * signed * signed * scale_of(mscale))
    unsigned = (scode[...].astype(F32) + 16.0) / 271.0
    old_s[...] = 0.999 * (unsigned * unsigned * scale_of(sscale))

    @pl.when(core == 1)
    def _():
        pl.semaphore_wait(barrier, 44)
        tell(far)

    @pl.when(core == 0)
    def _():
        pl.semaphore_wait(far, 1)

    along = []
    for k, d in enumerate(RING):
        own = pair(8 + k) * CODE
        crossing[k].wait_recv()
        both = own + x_code[d].astype(F32)
        if d:
            out_code[d] = to_codes(0.5 * both)
            c = remote(out_code.at[d], in_code.at[d], s_code.at[d], r_code.at[d], at(xh, zs[d], core))
            c.start()
            along.append(c)
    kept = both * (1.0 / CODE)

    group_at = [(ys[dy] + xls[dx], xls[dx] * 8 + ys[dy] // 2) for dy, dx in PEERS]
    group_from = [xls[dx] * 8 + back_ys[dy] // 2 for dy, dx in PEERS]
    own_eight = xl * 8 + y
    w_copies = [remote(w_out, w_in.at[i], s_w.at[i], r_w.at[i], (p, f)) for i, (p, _) in enumerate(group_at)]
    for c in w_copies:
        c.start()

    total = jnp.zeros((128, 128), jnp.int32)
    for c, d in zip(along, RING):
        c.wait_recv()
        total = total + in_code[d].astype(jnp.int32)
    total = total.astype(F32) * (2.0 / CODE) + kept
    for big in range(8):
        for r in range(2):
            summed[pl.ds(big * 16 + r, 8, stride=2), :] = total[big * 16 + r * 8 : big * 16 + r * 8 + 8]

    for c in small[4:]:
        c.wait()
    grad_sum = summed[...]
    moment = old_m[...] + 0.1 * grad_sum
    second = old_s[...] + 0.001 * grad_sum * grad_sum
    update = moment / (1.0 - 0.9**STEP) / (jnp.sqrt(second / (1.0 - 0.999**STEP)) + 1e-08)
    inner = master[...] + drift[...]
    pseudo = master[...] - (inner - 0.8 * (update + 0.025 * inner))
    weighted[...] = weight * pseudo

    def eight(p):
        return pl.ds(pl.multiple_of(p * 8, 8), 8)

    part_copies = [
        remote(weighted.at[eight(e)], part.at[i], s_part.at[i], r_part.at[i], (p, f))
        for i, (p, e) in enumerate(group_at)
    ]
    for c in part_copies:
        c.start()
    o_m[...] = moment
    o_s[...] = second
    all_weights = w_out[...]
    for i in range(15):
        w_copies[i].wait_recv()
        all_weights = all_weights + w_in[i]
    own_sum = weighted[eight(own_eight), :]
    for i in range(15):
        part_copies[i].wait_recv()
        own_sum = own_sum + part[i]
    own_mean = own_sum / all_weights

    def nesterov(at_rows, mean_pseudo):
        momentum = 0.9 * mom[at_rows, :] + mean_pseudo
        return master[at_rows, :] - 0.7 * (mean_pseudo + 0.9 * momentum), momentum

    fresh, _ = nesterov(eight(own_eight), own_mean)
    order[...] = fresh
    two = [order[pl.ds(r, 4, stride=2), :] for r in range(2)]
    slice_out[0] = jnp.concatenate(two, axis=0).astype(BF16)
    mean[eight(own_eight), :] = own_mean
    where = y * 8 + lax.rem(z, 4) * 2 + core
    slice_copies = []
    for n, (dy, dz) in enumerate(PLANE + ((0, 0),)):
        to = (ys[dy] + xl, xh * 16 + zs[dz] * 2 + z_half)
        copy = remote(slice_out.at[0], slice_in.at[where], s_slice.at[n], r_slice.at[where], to)
        slice_copies.append(copy)
        if n < 63:
            copy.start()
        else:
            pl.when(z_half != core)(copy.start)
            keep = pltpu.make_async_copy(slice_out.at[0], slice_in.at[where], r_slice.at[where])
            pl.when(z_half == core)(keep.start)

    mean_copies = []
    own_rows = mean.at[eight(own_eight)]
    for i, (p, _) in enumerate(group_at):
        c = remote(own_rows, own_rows, s_mean.at[i], r_mean.at[i], (p, f))
        c.start()
        mean_copies.append(c)

    x = xh * 2 + xl
    xs = [lax.rem(x + d, 4) for d in range(4)]

    def block(source_x, source_core, d):
        row = (source_x // 2 * 2 + source_core) * 16
        column = (lax.rem(source_x, 2) * 8 + ys[d] // 2) * 512
        return o_model.at[pl.ds(pl.multiple_of(row, 16), 16), pl.ds(pl.multiple_of(column, 512), 512)]

    sends = []
    for n, d in enumerate(reversed(RING)):
        from_y = ys[d] // 2
        for k in range(8):
            slot = from_y * 8 + k
            remote(slice_out.at[0], slice_in.at[slot], s_slice.at[0], r_slice.at[slot], sibling).wait_recv()
        arrived = slice_in[pl.ds(pl.multiple_of(from_y * 8, 8), 8)].astype(F32)
        sorted_rows[...] = arrived.reshape(64, 128)
        piece = block(x, core, d)
        for j in range(4):
            two = [sorted_rows[pl.ds(h * 32 + j, 8, stride=4), :] for h in range(2)]
            piece[:, j * 128 : j * 128 + 128] = jnp.concatenate(two, axis=0).astype(BF16)
        for dx in CROSS:
            to = (y * 2 + lax.rem(xs[dx], 2), xs[dx] // 2 * 16 + z * 2 + core)
            sends.append(remote(piece, piece, s_block.at[dx * 8 + n], r_block.at[dx * 8 + n], to))
            sends[-1].start()
        sends.append(remote(piece, piece, s_fwd.at[n], r_fwd.at[n], sibling))
        sends[-1].start()

    for i, e in enumerate(group_from):
        remote(mean.at[eight(e)], mean.at[eight(e)], s_mean.at[i], r_mean.at[i], sibling).wait_recv()
    everything = pl.ds(0, 128)
    o_master[...], o_mom[...] = nesterov(everything, mean[...])

    for c in swaps + crossing + along + w_copies + part_copies + mean_copies + slice_copies[:63]:
        c.wait_send()
    pl.when(z_half != core)(slice_copies[63].wait_send)

    for n, d in enumerate(reversed(RING)):
        for dx in CROSS:
            piece = block(xs[4 - dx], core, d)
            at_n = dx * 8 + n
            remote(piece, piece, s_block.at[at_n], r_block.at[at_n], sibling).wait_recv()
            sends.append(remote(piece, piece, s_fwd.at[at_n], r_fwd.at[at_n], sibling))
            sends[-1].start()
    for n, d in enumerate(reversed(RING)):
        for dx in (0,) + CROSS:
            piece = block(xs[(4 - dx) % 4], other, d)
            at_n = dx * 8 + n
            remote(piece, piece, s_fwd.at[at_n], r_fwd.at[at_n], sibling).wait_recv()
    for c in sends:
        c.wait_send()


def outer_step(*args):
    hbm = pl.BlockSpec(memory_space=pltpu.HBM)
    vmem = pl.BlockSpec(memory_space=pltpu.VMEM)
    square = pltpu.VMEM((128, 128), F32)
    codes = pltpu.VMEM((128, 128), jnp.int32)
    codes16 = pltpu.VMEM((8, 128, 128), jnp.int16)
    eight = lambda n: pltpu.VMEM((n, 8, 128), F32)
    dma = pltpu.SemaphoreType.DMA
    out = pltpu.VMEM((128, 128), F32)
    return pl.pallas_call(
        kernel,
        out_shape=(out, out, out, out, pltpu.VMEM((64, 8192), BF16)),
        in_specs=[hbm] * 8 + [pl.BlockSpec(memory_space=pltpu.SMEM)],
        out_specs=(vmem,) * 5,
        scratch_shapes=[
            pltpu.VMEM((64, 8192), BF16), pltpu.VMEM((16, 128, 128), BF16),
            square, square, square, codes, codes, pltpu.VMEM((1, 2, 32), F32), pltpu.VMEM((1, 2, 32), F32),
            pltpu.VMEM((1024, 128), F32), pltpu.VMEM((2, 16, 128, 128), BF16), codes16, codes16, codes16, codes16,
            square, square, square, square, eight(15), square,
            pltpu.VMEM((8, 128), F32), eight(15), pltpu.VMEM((8, 128), F32),
            pltpu.VMEM((1, 8, 128), BF16), pltpu.VMEM((64, 8, 128), BF16), pltpu.VMEM((64, 128), F32),
            dma((11,)), dma((16,)), dma((16,)), dma((8,)), dma((8,)), dma((8,)), dma((8,)), dma((15,)), dma((15,)), dma((15,)),
            dma((15,)), dma((15,)), dma((15,)), dma((64,)), dma((64,)), dma((32,)), dma((32,)), dma((32,)), dma((32,)),
            pltpu.SemaphoreType.REGULAR, pltpu.SemaphoreType.REGULAR,
        ],
        compiler_params=pltpu.CompilerParams(
            collective_id=0, has_side_effects=True, vmem_limit_bytes=16 * 1024 * 1024
        ),
        name="outer_step",
    )(*args)


def hand_over(*refs):
    sems = refs[-1]
    pairs = [(refs[4].at[pl.ds(16 * k, 16)], refs[9].at[pl.ds(16 * k, 16)]) for k in range(4)]
    pairs += [(refs[k], refs[5 + k]) for k in range(4)]
    copies = [pltpu.make_async_copy(a, b, sems.at[k]) for k, (a, b) in enumerate(pairs)]
    for c in copies:
        c.start()
    for c in copies:
        c.wait()


def on_device(grad_terms, master, inner_drift, momentum, moment_codes, second_codes, moment_scale, second_scale, counts):
    def to_flat(x):
        return x.reshape(2, 64, 128).transpose(1, 0, 2).reshape(128, 128)

    def from_flat(x):
        return x.reshape(64, 2, 128).transpose(1, 0, 2).reshape(2, 8192)

    operands = (
        grad_terms[0, 0], to_flat(master), to_flat(inner_drift), to_flat(momentum),
        to_flat(moment_codes), to_flat(second_codes), moment_scale, second_scale,
    )
    outs = outer_step(*(pltpu.with_memory_space_constraint(x, pltpu.HBM) for x in operands), counts)
    a, b, c, d, model = pl.pallas_call(
        hand_over,
        out_shape=tuple(jax.ShapeDtypeStruct(o.shape, o.dtype) for o in outs),
        in_specs=[pl.BlockSpec(memory_space=pltpu.VMEM)] * 5,
        out_specs=(pl.BlockSpec(memory_space=pltpu.HBM),) * 5,
        scratch_shapes=[pltpu.SemaphoreType.DMA((8,))],
        name="hand_over",
    )(*(pltpu.with_memory_space_constraint(o, pltpu.VMEM) for o in outs))
    return from_flat(a), from_flat(b), from_flat(c)[None], from_flat(d)[None], model


def solution(mesh):
    rows = P("fsdp", None)
    both = P("group", "fsdp", None)
    return jax.shard_map(
        on_device,
        mesh=mesh,
        in_specs=(P("group", "fsdp", None, None), rows, both, rows, both, both, both, both, P("group")),
        out_specs=(rows, rows, both, both, P()),
        check_vma=False,
    )
```

```python
import jax
import jax.numpy as jnp
from jax import lax
from jax.experimental import pallas as pl
from jax.experimental.pallas import tpu as pltpu
from jax.sharding import PartitionSpec as P

BLOCK = 256
STEP = 500
MESH = pl.DeviceIdType.MESH
F32 = jnp.float32
BF16 = jnp.bfloat16
CODE = 27408.0
RING = (4, 3, 5, 2, 6, 1, 7, 0)
PEERS = tuple((dy, dx) for dy in RING for dx in (1, 0))[:15]
PLANE = tuple((dy, dz) for dy in reversed(RING) for dz in RING if dy or dz)
CROSS = (2, 1, 3)


def kernel(
    grad, master_in, drift_in, mom_in, mcode_in, scode_in, mscale_in, sscale_in, counts,
    o_master, o_mom, o_m, o_s, o_model,
    terms, sib, master, drift, mom, mcode, scode, mscale, sscale,
    wide, by_owner, cross_code, out_code, x_code, in_code, summed, old_m, old_s, weighted, part, mean, w_out, w_in, order, slice_out, slice_in,
    sorted_rows, s_in, s_sib, r_sib, s_code, r_code, s_x, r_x, s_w, r_w, s_part, r_part, s_mean, r_mean, s_slice, r_slice,
    s_block, r_block, s_fwd, r_fwd, near, far,
):
    g = lax.axis_index("group")
    f = lax.axis_index("fsdp")
    y, xl = g // 2, g % 2
    xh, z, core = f // 16, (f // 2) % 8, f % 2
    other = 1 - core
    zs = [lax.rem(z + d, 8) for d in range(8)]
    ys = [lax.rem(y + d, 8) * 2 for d in range(8)]
    xls = [xl, 1 - xl]

    def at(px, pz, pc):
        return (g, px * 16 + pz * 2 + pc)

    sibling = at(xh, z, other)

    def remote(source, target, send, recv, device):
        return pltpu.make_async_remote_copy(
            source, target, send, recv, device_id=device, device_id_type=MESH
        )

    def all_sent(ref, sem):
        remote(ref, ref, sem.at[0], sem.at[0], sibling).wait_send()

    def all_arrived(ref, sem):
        remote(ref, ref, sem, sem, sibling).wait_recv()

    barrier = pltpu.get_barrier_semaphore()

    def greet(device):
        pl.semaphore_signal(barrier, inc=1, device_id=device, device_id_type=MESH)

    across_x = at(1 - xh, z, core)
    greet(at(1 - xh, z, 0))
    pl.when(core == 1)(lambda: greet(sibling))
    z_half = z // 4
    tiles = [px * 2 + pz for px in (1 - xh, xh) for pz in (1 - z_half, z_half)]

    def sixteen(t):
        return pl.ds(pl.multiple_of(t * 16, 16), 16)

    loads = [
        pltpu.make_async_copy(grad.at[sixteen(t)], terms.at[sixteen(t)], s_in.at[k]) for k, t in enumerate(tiles)
    ]
    small = [
        pltpu.make_async_copy(a, b, s_in.at[4 + k])
        for k, (a, b) in enumerate((
            (mscale_in, mscale), (sscale_in, sscale), (mcode_in, mcode), (scode_in, scode),
            (master_in, master), (drift_in, drift), (mom_in, mom),
        ))
    ]
    for c in loads + small:
        c.start()
    for d in RING[:7]:
        greet(at(xh, zs[d], 1))
    for dy, dx in PEERS:
        greet((ys[dy] + xls[dx], f + 1 - core))

    def tell(sem):
        pl.semaphore_signal(sem, inc=1, device_id=sibling, device_id_type=MESH)

    @pl.when(core == 0)
    def _():
        pl.semaphore_wait(barrier, 3)
        tell(near)

    def regroup(k):
        loads[k].wait()

        def widen(j, _):
            columns = pl.ds(pl.multiple_of(j * 128, 128), 128)
            wide[pl.ds(pl.multiple_of(j * 16, 16), 16), :] = terms[sixteen(tiles[k]), columns].astype(F32)
            return 0

        lax.fori_loop(0, 64, widen, 0, unroll=4)
        for q in range(4):
            for pc in range(2):
                for big in range(8):
                    two = [wide[pl.ds(big * 128 + q * 4 + pc * 2 + r, 8, stride=16), :] for r in range(2)]
                    by_owner[pc, tiles[k] * 4 + q, big * 16 : big * 16 + 16, :] = jnp.concatenate(two, axis=0).astype(
                        BF16
                    )

    chips = [(1 - xh) * 8 + zs[d] for d in RING] + [xh * 8 + zs[d] for d in RING]
    swaps = [
        remote(by_owner.at[other, chip], sib.at[k], s_sib.at[0], r_sib.at[k], sibling)
        for k, chip in enumerate(chips)
    ]

    regroup(0)
    regroup(1)

    @pl.when(core == 1)
    def _():
        pl.semaphore_wait(near, 1)

    for c in swaps[:8]:
        c.start()
    regroup(2)
    regroup(3)

    def pair(k):
        swaps[k].wait_recv()
        return by_owner[core, chips[k]].astype(F32) + sib[k].astype(F32)

    def to_codes(values):
        return jnp.round(values).astype(jnp.int32).astype(jnp.int16)

    crossing = []
    for k, d in enumerate(RING):
        cross_code[d] = to_codes(pair(k) * CODE)
        c = remote(cross_code.at[d], x_code.at[d], s_x.at[0], r_x.at[d], across_x)
        c.start()
        crossing.append(c)
        swaps[8 + k].start()

    for c in small[:4]:
        c.wait()
    weight = counts[0].astype(F32)
    w_out[...] = jnp.full((8, 128), weight, F32)
    rows = lax.broadcasted_iota(jnp.int32, (128, 32), 0)
    hit = lax.broadcasted_iota(jnp.int32, (128, 32), 1) == rows // 4

    def scale_of(ref):
        both = jnp.where(rows % 2 == 0, ref[0, 0:1, :], ref[0, 1:2, :])
        return jnp.sum(jnp.where(hit, both, 0.0), axis=1, keepdims=True)

    signed = (mcode[...].astype(F32) - 127.5) / 127.5
    old_m[...] = 0.9 * (signed * signed * signed * scale_of(mscale))
    unsigned = (scode[...].astype(F32) + 16.0) / 271.0
    old_s[...] = 0.999 * (unsigned * unsigned * scale_of(sscale))

    @pl.when(core == 1)
    def _():
        pl.semaphore_wait(barrier, 44)
        tell(far)

    @pl.when(core == 0)
    def _():
        pl.semaphore_wait(far, 1)

    along = []
    for k, d in enumerate(RING):
        own = pair(8 + k) * CODE
        crossing[k].wait_recv()
        both = own + x_code[d].astype(F32)
        if d:
            out_code[d] = to_codes(0.5 * both)
            c = remote(out_code.at[d], in_code.at[d], s_code.at[0], r_code.at[d], at(xh, zs[d], core))
            c.start()
            along.append(c)
    kept = both * (1.0 / CODE)

    group_at = [(ys[dy] + xls[dx], xls[dx] * 8 + ys[dy] // 2) for dy, dx in PEERS]
    own_eight = xl * 8 + y
    w_copies = [remote(w_out, w_in.at[i], s_w.at[0], r_w.at[0], (p, f)) for i, (p, _) in enumerate(group_at)]
    for c in w_copies:
        c.start()

    total = jnp.zeros((128, 128), jnp.int32)
    for c, d in zip(along, RING):
        c.wait_recv()
        total = total + in_code[d].astype(jnp.int32)
    total = total.astype(F32) * (2.0 / CODE) + kept
    for big in range(8):
        for r in range(2):
            summed[pl.ds(big * 16 + r, 8, stride=2), :] = total[big * 16 + r * 8 : big * 16 + r * 8 + 8]

    for c in small[4:]:
        c.wait()
    grad_sum = summed[...]
    moment = old_m[...] + 0.1 * grad_sum
    second = old_s[...] + 0.001 * grad_sum * grad_sum
    update = moment / (1.0 - 0.9**STEP) / (jnp.sqrt(second / (1.0 - 0.999**STEP)) + 1e-08)
    inner = master[...] + drift[...]
    pseudo = master[...] - (inner - 0.8 * (update + 0.025 * inner))
    weighted[...] = weight * pseudo

    def eight(p):
        return pl.ds(pl.multiple_of(p * 8, 8), 8)

    part_copies = [
        remote(weighted.at[eight(e)], part.at[i], s_part.at[0], r_part.at[0], (p, f))
        for i, (p, e) in enumerate(group_at)
    ]
    for c in part_copies:
        c.start()
    o_m[...] = moment
    o_s[...] = second
    all_weights = w_out[...]
    all_arrived(w_in, r_w.at[0])
    for i in range(15):
        all_weights = all_weights + w_in[i]
    own_sum = weighted[eight(own_eight), :]
    all_arrived(part, r_part.at[0])
    for i in range(15):
        own_sum = own_sum + part[i]
    own_mean = own_sum / all_weights

    def nesterov(at_rows, mean_pseudo):
        momentum = 0.9 * mom[at_rows, :] + mean_pseudo
        return master[at_rows, :] - 0.7 * (mean_pseudo + 0.9 * momentum), momentum

    fresh, _ = nesterov(eight(own_eight), own_mean)
    order[...] = fresh
    two = [order[pl.ds(r, 4, stride=2), :] for r in range(2)]
    slice_out[0] = jnp.concatenate(two, axis=0).astype(BF16)
    mean[eight(own_eight), :] = own_mean
    where = y * 8 + lax.rem(z, 4) * 2 + core
    slice_copies = []
    for n, (dy, dz) in enumerate(PLANE + ((0, 0),)):
        to = (ys[dy] + xl, xh * 16 + zs[dz] * 2 + z_half)
        copy = remote(slice_out.at[0], slice_in.at[where], s_slice.at[0], r_slice.at[y], to)
        slice_copies.append(copy)
        if n < 63:
            copy.start()
        else:
            pl.when(z_half != core)(copy.start)
            keep = pltpu.make_async_copy(slice_out.at[0], slice_in.at[where], r_slice.at[y])
            pl.when(z_half == core)(keep.start)

    mean_copies = []
    own_rows = mean.at[eight(own_eight)]
    for i, (p, _) in enumerate(group_at):
        c = remote(own_rows, own_rows, s_mean.at[0], r_mean.at[0], (p, f))
        c.start()
        mean_copies.append(c)

    x = xh * 2 + xl
    xs = [lax.rem(x + d, 4) for d in range(4)]

    def block(source_x, source_core, d):
        row = (source_x // 2 * 2 + source_core) * 16
        column = (lax.rem(source_x, 2) * 8 + ys[d] // 2) * 512
        return o_model.at[pl.ds(pl.multiple_of(row, 16), 16), pl.ds(pl.multiple_of(column, 512), 512)]

    for n, d in enumerate(reversed(RING)):
        from_y = ys[d] // 2
        slots = pl.ds(pl.multiple_of(from_y * 8, 8), 8)
        all_arrived(slice_in.at[slots], r_slice.at[from_y])
        arrived = slice_in[slots].astype(F32)
        sorted_rows[...] = arrived.reshape(64, 128)
        piece = block(x, core, d)
        for j in range(4):
            two = [sorted_rows[pl.ds(h * 32 + j, 8, stride=4), :] for h in range(2)]
            piece[:, j * 128 : j * 128 + 128] = jnp.concatenate(two, axis=0).astype(BF16)
        for dx in CROSS:
            to = (y * 2 + lax.rem(xs[dx], 2), xs[dx] // 2 * 16 + z * 2 + core)
            remote(piece, piece, s_block.at[0], r_block.at[dx * 8 + n], to).start()
        remote(piece, piece, s_fwd.at[0], r_fwd.at[0], sibling).start()

    fifteen = mean.at[pl.ds(0, 120)]
    all_arrived(fifteen, r_mean.at[0])
    everything = pl.ds(0, 128)
    o_master[...], o_mom[...] = nesterov(everything, mean[...])

    all_sent(sib, s_sib)
    all_sent(cross_code, s_x)
    all_sent(out_code.at[pl.ds(0, 7)], s_code)
    all_sent(w_in, s_w)
    all_sent(part, s_part)
    all_sent(fifteen, s_mean)
    all_sent(slice_in.at[pl.ds(0, 63)], s_slice)
    pl.when(z_half != core)(slice_copies[63].wait_send)

    for n, d in enumerate(reversed(RING)):
        for dx in CROSS:
            piece = block(xs[4 - dx], core, d)
            at_n = dx * 8 + n
            remote(piece, piece, s_block.at[0], r_block.at[at_n], sibling).wait_recv()
            remote(piece, piece, s_fwd.at[0], r_fwd.at[0], sibling).start()
    all_sent(o_model.at[pl.ds(0, 48), pl.ds(0, 4096)], s_block)
    rows_32 = o_model.at[pl.ds(0, 32)]
    all_arrived(rows_32, r_fwd.at[0])
    all_sent(rows_32, s_fwd)


def outer_step(*args):
    hbm = pl.BlockSpec(memory_space=pltpu.HBM)
    vmem = pl.BlockSpec(memory_space=pltpu.VMEM)
    square = pltpu.VMEM((128, 128), F32)
    codes = pltpu.VMEM((128, 128), jnp.int32)
    codes16 = pltpu.VMEM((8, 128, 128), jnp.int16)
    eight = lambda n: pltpu.VMEM((n, 8, 128), F32)
    dma = pltpu.SemaphoreType.DMA
    one = dma((1,))
    out = pltpu.VMEM((128, 128), F32)
    return pl.pallas_call(
        kernel,
        out_shape=(out, out, out, out, pltpu.VMEM((64, 8192), BF16)),
        in_specs=[hbm] * 8 + [pl.BlockSpec(memory_space=pltpu.SMEM)],
        out_specs=(vmem,) * 5,
        scratch_shapes=[
            pltpu.VMEM((64, 8192), BF16), pltpu.VMEM((16, 128, 128), BF16),
            square, square, square, codes, codes, pltpu.VMEM((1, 2, 32), F32), pltpu.VMEM((1, 2, 32), F32),
            pltpu.VMEM((1024, 128), F32), pltpu.VMEM((2, 16, 128, 128), BF16), codes16, codes16, codes16, codes16,
            square, square, square, square, eight(15), square,
            pltpu.VMEM((8, 128), F32), eight(15), pltpu.VMEM((8, 128), F32),
            pltpu.VMEM((1, 8, 128), BF16), pltpu.VMEM((64, 8, 128), BF16), pltpu.VMEM((64, 128), F32),
            dma((11,)), one, dma((16,)), one, dma((8,)), one, dma((8,)), one, one, one, one, one, one, one, dma((8,)),
            one, dma((32,)), one, one,
            pltpu.SemaphoreType.REGULAR, pltpu.SemaphoreType.REGULAR,
        ],
        compiler_params=pltpu.CompilerParams(
            collective_id=0, has_side_effects=True, vmem_limit_bytes=16 * 1024 * 1024
        ),
        name="outer_step",
    )(*args)


def hand_over(*refs):
    sems = refs[-1]
    pairs = [(refs[4].at[pl.ds(16 * k, 16)], refs[9].at[pl.ds(16 * k, 16)]) for k in range(4)]
    pairs += [(refs[k], refs[5 + k]) for k in range(4)]
    copies = [pltpu.make_async_copy(a, b, sems.at[k]) for k, (a, b) in enumerate(pairs)]
    for c in copies:
        c.start()
    for c in copies:
        c.wait()


def on_device(grad_terms, master, inner_drift, momentum, moment_codes, second_codes, moment_scale, second_scale, counts):
    def to_flat(x):
        return x.reshape(2, 64, 128).transpose(1, 0, 2).reshape(128, 128)

    def from_flat(x):
        return x.reshape(64, 2, 128).transpose(1, 0, 2).reshape(2, 8192)

    operands = (
        grad_terms[0, 0], to_flat(master), to_flat(inner_drift), to_flat(momentum),
        to_flat(moment_codes), to_flat(second_codes), moment_scale, second_scale,
    )
    outs = outer_step(*(pltpu.with_memory_space_constraint(x, pltpu.HBM) for x in operands), counts)
    a, b, c, d, model = pl.pallas_call(
        hand_over,
        out_shape=tuple(jax.ShapeDtypeStruct(o.shape, o.dtype) for o in outs),
        in_specs=[pl.BlockSpec(memory_space=pltpu.VMEM)] * 5,
        out_specs=(pl.BlockSpec(memory_space=pltpu.HBM),) * 5,
        scratch_shapes=[pltpu.SemaphoreType.DMA((8,))],
        name="hand_over",
    )(*(pltpu.with_memory_space_constraint(o, pltpu.VMEM) for o in outs))
    return from_flat(a), from_flat(b), from_flat(c)[None], from_flat(d)[None], model


def solution(mesh):
    rows = P("fsdp", None)
    both = P("group", "fsdp", None)
    return jax.shard_map(
        on_device,
        mesh=mesh,
        in_specs=(P("group", "fsdp", None, None), rows, both, rows, both, both, both, both, P("group")),
        out_specs=(rows, rows, both, both, P()),
        check_vma=False,
    )
```
